32 devices in a mesh: heads: 4 (over y, x), ctx: 8 (over z, core).
Axes of the slice: x: 2, y: 2, z: 4, core: 2. Of those that a mesh axis runs over, the one named last changes fastest.
Arguments:
- queries: bfloat16 [3072, 8192], P('ctx', 'heads'), may hold values from -20 to 20
- keys: bfloat16 [3072, 1024], P('ctx', 'heads'), may hold values from -20 to 20
- values: bfloat16 [3072, 1024], P('ctx', 'heads'), may hold values from -6 to 6
- positions: int32 [3072], P('ctx'), may hold values from 0 to 4607, as said below
Outputs:
- attended: bfloat16 [3072, 8192], P(('ctx', 'heads'))
The draws below stay inside these ranges and needn't reach their ends.
Inputs may be any that keep to these rules, and one draw needn't show every extreme that they name: `positions`: positions start at 0 at the first token and rise by 1 or 2 from each token to the next; exactly 1536 of these steps rise by 2.
All inputs are finite; a program needn't handle non-finite values.
Results may differ from the reference program's by a relative error of at most 0.0092.
Values may be sent and summed in bfloat16 or wider, within the bound.
No kernel may reach another device: no remote copies, remote signals or barrier semaphores. Data moves between devices by JAX's collectives and lax.ppermute only.
A program may use at most 64 MiB of HBM per device.

```python
import math
import jax
import jax.numpy as jnp
from jax import lax

QH = 64
KVH = 8
HD = 128
GROUP = 8
TOKENS = 3072


def draw_queries(key, part):
    drawn = jax.random.truncated_normal(jax.random.fold_in(key, 1), -6.0, 6.0, (TOKENS, QH * HD), jnp.float32) * 1.2
    return drawn.astype(jnp.bfloat16)


def draw_keys(key, part):
    drawn = jax.random.truncated_normal(jax.random.fold_in(key, 2), -6.0, 6.0, (TOKENS, KVH * HD), jnp.float32) * 2.0
    return drawn.astype(jnp.bfloat16)


def draw_positions(key, part):
    order_table = jax.random.permutation(jax.random.fold_in(key, 3), TOKENS - 1)
    step_table = 1 + (order_table < TOKENS // 2).astype(jnp.int32)
    rising = jnp.cumsum(step_table).astype(jnp.int32)
    return jnp.concatenate([jnp.zeros((1,), jnp.int32), rising], 0).astype(jnp.int32)


def level_of(own_key, shape, pieces, smallest, largest):
    factor_of, own = 1.0, jax.random.fold_in(own_key, 6)
    for dim, blocks in pieces:
        heights = jnp.exp(jax.random.uniform(jax.random.fold_in(own, dim), (blocks,), jnp.float32, smallest / len(pieces), largest / len(pieces)))
        factor_of = factor_of * jnp.repeat(heights, shape[dim] // blocks).reshape([-1 if axis == dim else 1 for axis in range(len(shape))])
    return factor_of


def centred(stream_key, extent, deviation, bound, split=(), kind=jnp.bfloat16):
    values = deviation * jax.random.normal(stream_key, extent, jnp.float32)
    if split:
        values = values * level_of(stream_key, extent, split, -0.22, 0.18)
    return jnp.clip(values, -bound, bound).astype(kind)


def setup_inputs(seed: int = 0) -> dict:
    key_of = jax.random.split(jax.random.key(seed), 5)
    queries = draw_queries(jax.random.fold_in(key_of[4], 71), 0)
    keys = draw_keys(jax.random.fold_in(key_of[4], 71), 0)
    values = centred(key_of[2], (TOKENS, KVH * HD), 1.0, 6.0, ((0, 8), (1, 4)))
    positions = draw_positions(jax.random.fold_in(key_of[4], 71), 0)
    return {"queries": queries, "keys": keys, "values": values, "positions": positions}


def rotary_tables(positions, head_dim):
    step_index = jnp.arange(head_dim // 2, dtype=jnp.float32)
    base_freq = jnp.power(jnp.float32(500000.0), -(2.0 * step_index / head_dim))
    wavelen = 2.0 * math.pi / base_freq
    blend_factor = (8192.0 / wavelen - 1.0) / 3.0
    middle = (1.0 - blend_factor) * base_freq / 8.0 + blend_factor * base_freq
    inv_freq = jnp.where(wavelen < 2048.0, base_freq, jnp.where(wavelen > 8192.0, base_freq / 8.0, middle))
    angles = positions.astype(jnp.float32)[:, None] * inv_freq[None, :]
    return (jnp.cos(angles), jnp.sin(angles))

def rotate(head_data, cosine, sine_table):
    halfway = head_data.shape[-1] // 2
    first_part = head_data[..., :halfway]
    second = head_data[..., halfway:]
    cos_rows = cosine[:, None, :]
    sin_rows = sine_table[:, None, :]
    return jnp.concatenate([first_part * cos_rows - second * sin_rows, second * cos_rows + first_part * sin_rows], axis=-1)

def reference(queries, keys, values, positions):
    cosine, sine_table = rotary_tables(positions, HD)
    rot_queries = rotate(queries.astype(jnp.float32).reshape(TOKENS, QH, HD), cosine, sine_table).astype(jnp.bfloat16)
    rot_keys = rotate(keys.astype(jnp.float32).reshape(TOKENS, KVH, HD), cosine, sine_table).astype(jnp.bfloat16)
    query_groups = rot_queries.reshape(TOKENS, KVH, GROUP, HD)
    value_heads = values.reshape(TOKENS, KVH, HD)
    block_rows = math.gcd(TOKENS, 512)
    count_blocks = TOKENS // block_rows
    scale_value = 1.0 / math.sqrt(HD)
    key_index = jnp.arange(TOKENS, dtype=jnp.int32)

    def per_head(head_index):
        keys_one = lax.dynamic_index_in_dim(rot_keys, head_index, 1, keepdims=False).astype(jnp.float32)
        values_one = lax.dynamic_index_in_dim(value_heads, head_index, 1, keepdims=False).astype(jnp.float32)
        queries_one = lax.dynamic_index_in_dim(query_groups, head_index, 1, keepdims=False)

        def per_block(block_index):
            block_start = (block_index * block_rows).astype(jnp.int32)
            query_block = lax.dynamic_slice_in_dim(queries_one, block_start, block_rows, 0).astype(jnp.float32)
            scores = jnp.einsum('qgd,kd->gqk', query_block, keys_one, precision=lax.Precision.HIGHEST) * scale_value
            query_index = block_start + jnp.arange(block_rows, dtype=jnp.int32)
            allowed = key_index[None, :] <= query_index[:, None]
            scores = jnp.where(allowed[None], scores, -jnp.inf)
            row_max = lax.optimization_barrier(jnp.max(scores, axis=-1, keepdims=True))
            weights = jnp.exp(scores - row_max)
            total_sum = lax.optimization_barrier(jnp.sum(weights, axis=-1))
            rounded = lax.optimization_barrier(weights.astype(jnp.bfloat16)).astype(jnp.float32)
            mixed_values = jnp.einsum('gqk,kd->qgd', rounded, values_one, precision=lax.Precision.HIGHEST)
            return mixed_values / jnp.transpose(total_sum)[:, :, None]
        return lax.map(per_block, jnp.arange(count_blocks, dtype=jnp.int32))
    result = lax.map(per_head, jnp.arange(KVH, dtype=jnp.int32))
    result = jnp.transpose(result, (1, 2, 0, 3, 4)).reshape(TOKENS, QH * HD)
    return result.astype(jnp.bfloat16)
```

```python
import functools
import math

import jax
import jax.numpy as jnp
import numpy as np
from jax import lax
from jax.experimental import pallas as pl
from jax.experimental.pallas import tpu as pltpu
from jax.sharding import PartitionSpec as P

HD = 128
HALF = HD // 2
NEG_FILL = -1e30
EXP2_SCALE = math.log2(math.e) / math.sqrt(HD)


def inverse_frequencies():
    base = 500000.0 ** (-2.0 * np.arange(HALF) / HD)
    wave = 2.0 * math.pi / base
    blend = (8192.0 / wave - 1.0) / 3.0
    middle = (1.0 - blend) * base / 8.0 + blend * base
    freq = np.where(wave < 2048.0, base, np.where(wave > 8192.0, base / 8.0, middle))
    return np.concatenate([freq, freq]).astype(np.float32)[None, :]


def cos_sin(angle):
    turns = jnp.round(angle * (2.0 / math.pi))
    rest = angle - turns * 1.5703125
    rest = rest - turns * 4.837512969970703e-4
    rest = rest - turns * 7.54978995489188e-8
    quadrant = turns.astype(jnp.int32) & 3
    sq = rest * rest
    sine = rest + rest * sq * (-1.6666654611e-1 + sq * (8.3321608736e-3 - sq * 1.9515295891e-4))
    cosine = (
        1.0
        - 0.5 * sq
        + sq * sq * (4.166664568298827e-2 + sq * (-1.388731625493765e-3 + sq * 2.443315711809948e-5))
    )
    odd = (quadrant & 1) == 1
    cos_out = jnp.where(odd, sine, cosine)
    sin_out = jnp.where(odd, cosine, sine)
    cos_out = jnp.where((quadrant == 1) | (quadrant == 2), -cos_out, cos_out)
    sin_out = jnp.where(quadrant >= 2, -sin_out, sin_out)
    return cos_out, sin_out


def rotate(x, cosine, sine):
    return x * cosine + pltpu.roll(x, HALF, 1) * sine


def prep_kernel(heads, pos_ref, freq_ref, k_ref, v_ref, table_ref, *pack_refs):
    sign = jnp.where(lax.broadcasted_iota(jnp.int32, (HD, HD), 1) < HALF, -1.0, 1.0)
    for tile in range(k_ref.shape[0] // HD):
        rows = slice(tile * HD, (tile + 1) * HD)
        pos = pos_ref[:, rows].astype(jnp.float32)
        pos = jnp.broadcast_to(pos, (HD, HD)).T
        cosine, sine = cos_sin(pos * freq_ref[...])
        sine = sine * sign
        table_ref[rows, :HD] = cosine
        table_ref[rows, HD:] = sine
        for head in range(heads):
            cols = slice(head * HD, (head + 1) * HD)
            key = rotate(k_ref[rows, cols].astype(jnp.float32), cosine, sine)
            pack_refs[head][rows, :HD] = key.astype(jnp.bfloat16)
            pack_refs[head][rows, HD:] = v_ref[rows, cols].T


def prep(keys, values, positions):
    rows, cols = keys.shape
    heads = cols // HD
    return pl.pallas_call(
        functools.partial(prep_kernel, heads),
        out_shape=[jax.ShapeDtypeStruct((rows, 2 * HD), jnp.float32)]
        + [jax.ShapeDtypeStruct((rows, 2 * HD), jnp.bfloat16)] * heads,
        compiler_params=pltpu.CompilerParams(vmem_limit_bytes=32 << 20),
        name="prep",
    )(positions.reshape(1, rows), jnp.asarray(inverse_frequencies()), keys, values)


def flash_kernel(blocks, group, parts, q_ref, table_ref, *refs):
    kv_refs, out_refs = refs[:blocks], refs[blocks:]
    rows = q_ref.shape[0]
    piece = rows // parts
    me = lax.axis_index("heads")
    rank = lax.axis_index("ctx")
    chip, core = rank // 2, rank % 2
    query_cols, row_index = [], []
    starts = [pl.multiple_of((me ^ k) * piece, piece) for k in range(parts)]
    lane = lax.broadcasted_iota(jnp.int32, (1, piece), 1)
    for start in starts:
        row_index.append(lane + start)
    row_index = jnp.concatenate(row_index, axis=1)
    pieces = [q_ref[pl.ds(start, piece), :].astype(jnp.float32) for start in starts]
    queries = jnp.concatenate(pieces, axis=0)
    tables = jnp.concatenate([table_ref[pl.ds(start, piece), :] for start in starts], axis=0)
    for head in range(group):
        x = queries[:, head * HD : (head + 1) * HD]
        x = rotate(x, tables[:, :HD], tables[:, HD:])
        query_cols.append(x.T.astype(jnp.bfloat16))
    pair = 2 if group % 2 == 0 else 1
    tiles = [
        jnp.concatenate(query_cols[i : i + pair], axis=1) if pair > 1 else query_cols[i]
        for i in range(0, group, pair)
    ]
    tile_index = jnp.concatenate([row_index] * pair, axis=1)
    width = rows * pair
    work = [(b, i) for b in range(blocks) for i in range(len(tiles))]
    key_index = lax.broadcasted_iota(jnp.int32, (rows, width), 0)

    def score(b, i):
        return jnp.dot(kv_refs[b][:, :HD], tiles[i], preferred_element_type=jnp.float32)

    states = [None] * len(tiles)
    upcoming = score(*work[0])
    for step, (b, i) in enumerate(work):
        s = upcoming
        if step + 1 < len(work):
            upcoming = score(*work[step + 1])
        valid = None
        if b < 2:
            shift = 0 if b == 0 else jnp.where(core == 1, -rows, rows)
            s = jnp.where(key_index + shift <= tile_index, s, NEG_FILL)
        else:
            valid = chip >= b // 2
        top = jnp.max(s, axis=0, keepdims=True)
        values_t = jnp.concatenate(
            [kv_refs[b][t * HD : (t + 1) * HD, HD:] for t in range(rows // HD)], axis=1
        )
        if b == 0:
            p = jnp.exp2((s - top) * EXP2_SCALE)
            total = jnp.sum(p, axis=0, keepdims=True)
            acc = jnp.dot(values_t, p.astype(jnp.bfloat16), preferred_element_type=jnp.float32)
            states[i] = (top, total, acc)
            continue
        prev_top, total, acc = states[i]
        new_top = jnp.maximum(prev_top, top)
        p = jnp.exp2(s * EXP2_SCALE - new_top * EXP2_SCALE)
        part = jnp.sum(p, axis=0, keepdims=True)
        mixed = jnp.dot(values_t, p.astype(jnp.bfloat16), preferred_element_type=jnp.float32)
        factor = jnp.exp2((prev_top - new_top) * EXP2_SCALE)
        if valid is not None:
            factor = jnp.where(valid, factor, 1.0)
            part = jnp.where(valid, part, 0.0)
            new_top = jnp.where(valid, new_top, prev_top)
        states[i] = (new_top, total * factor + part, acc * factor + mixed)
    for i, (_, total, acc) in enumerate(states):
        result = acc * (1.0 / total)
        for g in range(pair):
            head = i * pair + g
            block = result[:, g * rows : (g + 1) * rows].T.astype(jnp.bfloat16)
            for k in range(parts):
                out_refs[k][:, head * HD : (head + 1) * HD] = block[k * piece : (k + 1) * piece]


def flash(queries, table, blocks, first, count, group, parts):
    rows = queries.shape[0]
    keys = sum(b.shape[0] for b in blocks)
    whole = lambda i: (0, 0)
    return pl.pallas_call(
        functools.partial(flash_kernel, len(blocks), group, parts),
        grid=(count // group,),
        in_specs=[
            pl.BlockSpec((rows, group * HD), lambda i: (0, first // group + i)),
            pl.BlockSpec(table.shape, whole),
        ]
        + [pl.BlockSpec(b.shape, whole) for b in blocks],
        out_specs=[pl.BlockSpec((rows // parts, group * HD), lambda i: (0, i))] * parts,
        out_shape=[jax.ShapeDtypeStruct((rows // parts, count * HD), jnp.bfloat16)] * parts,
        compiler_params=pltpu.CompilerParams(vmem_limit_bytes=40 << 20),
        cost_estimate=pl.CostEstimate(
            flops=4 * rows * count * keys * HD,
            bytes_accessed=4 * rows * count * HD + 4 * keys * HD,
            transcendentals=rows * count * keys,
        ),
        name="flash",
    )(queries, table, *blocks)


def place_kernel(heads, parts, *refs):
    pieces, out_ref, sems = refs[: heads * parts], refs[-2], refs[-1]
    me = lax.axis_index("heads")
    copies = []
    for head in range(heads):
        for k in range(parts):
            src = pieces[head * parts + k]
            cols = src.shape[1]
            start = pl.multiple_of(((me ^ k) * heads + head) * cols, cols)
            copies.append(
                pltpu.make_async_copy(src, out_ref.at[:, pl.ds(start, cols)], sems.at[len(copies)])
            )
    for c in copies:
        c.start()
    for c in copies:
        c.wait()


def place(pieces, heads, parts):
    rows, cols = pieces[0].shape
    return pl.pallas_call(
        functools.partial(place_kernel, heads, parts),
        in_specs=[pl.BlockSpec(memory_space=pltpu.VMEM)] * len(pieces),
        out_specs=pl.BlockSpec(memory_space=pl.ANY),
        out_shape=jax.ShapeDtypeStruct((rows, cols * len(pieces)), jnp.bfloat16),
        compiler_params=pltpu.CompilerParams(vmem_limit_bytes=16 << 20),
        scratch_shapes=[pltpu.SemaphoreType.DMA((len(pieces),))],
        name="place",
    )(*pieces)


def local(ctx_size, parts, queries, keys, values, positions):
    kv_heads = keys.shape[1] // HD
    group_size = queries.shape[1] // (kv_heads * HD)
    chips = ctx_size // 2
    up = [(c, c + 2) for c in range(ctx_size - 2)]
    swap = [(c, c ^ 1) for c in range(ctx_size)]
    table, *packs = prep(keys, values, positions)
    pieces = []
    for head in range(kv_heads):
        block = packs[head]
        blocks = [block, lax.ppermute(block, "ctx", swap)]
        for _ in range(1, chips):
            block = lax.ppermute(block, "ctx", up)
            blocks += [block, lax.ppermute(block, "ctx", swap)]
        outs = flash(queries, table, blocks, head * group_size, group_size, group_size // 2, parts)
        for k in range(parts):
            perm = [(i, i ^ k) for i in range(parts)]
            pieces.append(lax.ppermute(outs[k], "heads", perm) if k else outs[k])
    return place(pieces, kv_heads, parts)


def solution(mesh):
    return jax.shard_map(
        functools.partial(local, mesh.shape["ctx"], mesh.shape["heads"]),
        mesh=mesh,
        in_specs=(P("ctx", "heads"), P("ctx", "heads"), P("ctx", "heads"), P("ctx")),
        out_specs=P(("ctx", "heads"), None),
        check_vma=False,
    )
```

```python
import functools
import math

import jax
import jax.numpy as jnp
import numpy as np
from jax import lax
from jax.experimental import pallas as pl
from jax.experimental.pallas import tpu as pltpu
from jax.sharding import PartitionSpec as P

HD = 128
HALF = HD // 2
NEG_FILL = -1e30
EXP2_SCALE = math.log2(math.e) / math.sqrt(HD)
TOTAL_LIMIT = 2.0**100
TILE = 1536
ONES = 16
LIMIT = 24 << 20


def inverse_frequencies():
    base = 500000.0 ** (-2.0 * np.arange(HALF) / HD)
    wave = 2.0 * math.pi / base
    blend = (8192.0 / wave - 1.0) / 3.0
    middle = (1.0 - blend) * base / 8.0 + blend * base
    return np.where(wave < 2048.0, base, np.where(wave > 8192.0, base / 8.0, middle)).astype(np.float32)


def frequency_row():
    lane = lax.broadcasted_iota(jnp.int32, (1, HD), 1) % HALF
    row = jnp.zeros((1, HD), jnp.float32)
    for i, freq in enumerate(inverse_frequencies()):
        row = jnp.where(lane == i, float(freq), row)
    return row


def cos_sin(angle):
    turns = jnp.round(angle * (2.0 / math.pi))
    rest = angle - turns * 1.5703125
    rest = rest - turns * 4.837512969970703e-4
    rest = rest - turns * 7.54978995489188e-8
    quadrant = turns.astype(jnp.int32) & 3
    sq = rest * rest
    sine = rest + rest * sq * (-1.6666654611e-1 + sq * (8.3321608736e-3 - sq * 1.9515295891e-4))
    cosine = (
        1.0
        - 0.5 * sq
        + sq * sq * (4.166664568298827e-2 + sq * (-1.388731625493765e-3 + sq * 2.443315711809948e-5))
    )
    odd = (quadrant & 1) == 1
    cos_out = jnp.where(odd, sine, cosine)
    sin_out = jnp.where(odd, cosine, sine)
    cos_out = jnp.where((quadrant == 1) | (quadrant == 2), -cos_out, cos_out)
    sin_out = jnp.where(quadrant >= 2, -sin_out, sin_out)
    return cos_out, sin_out


def rotate(x, cosine, sine):
    return x * cosine + pltpu.roll(x, HALF, 1) * sine


def prep_kernel(heads, pos_hbm, k_hbm, v_hbm, table_ref, *refs):
    pack_refs, (pos_ref, k_ref, v_ref, sems) = refs[:heads], refs[heads:]
    pairs = [(pos_hbm, pos_ref), (k_hbm, k_ref), (v_hbm, v_ref)]
    loads = [pltpu.make_async_copy(src, dst, sems.at[i]) for i, (src, dst) in enumerate(pairs)]
    for load in loads:
        load.start()
    freq = frequency_row()
    loads[0].wait()
    tiles = [slice(t * HD, (t + 1) * HD) for t in range(k_ref.shape[0] // HD)]
    sign = jnp.where(lax.broadcasted_iota(jnp.int32, (HD, HD), 1) < HALF, -1.0, 1.0)
    tables = []
    for rows in tiles:
        pos = pos_ref[rows].reshape(1, HD).astype(jnp.float32)
        pos = jnp.broadcast_to(pos, (HD, HD)).T
        cosine, sine = cos_sin(pos * freq)
        sine = sine * sign
        table_ref[rows, :HD] = cosine
        table_ref[rows, HD:] = sine
        tables.append((cosine, sine))
    for load in loads[1:]:
        load.wait()
    for rows, (cosine, sine) in zip(tiles, tables, strict=True):
        for head in range(heads):
            cols = slice(head * HD, (head + 1) * HD)
            key = rotate(k_ref[rows, cols].astype(jnp.float32), cosine, sine)
            pack_refs[head][rows, :HD] = key.astype(jnp.bfloat16)
            pack_refs[head][rows, HD:] = v_ref[rows, cols].T


def prep(keys, values, positions):
    rows, cols = keys.shape
    heads = cols // HD
    vmem, hbm = pl.BlockSpec(memory_space=pltpu.VMEM), pl.BlockSpec(memory_space=pltpu.HBM)
    return pl.pallas_call(
        functools.partial(prep_kernel, heads),
        in_specs=[hbm] * 3,
        out_specs=[vmem] * (1 + heads),
        out_shape=[jax.ShapeDtypeStruct((rows, 2 * HD), jnp.float32)]
        + [jax.ShapeDtypeStruct((rows, 2 * HD), jnp.bfloat16)] * heads,
        scratch_shapes=[
            pltpu.VMEM(positions.shape, positions.dtype),
            pltpu.VMEM(keys.shape, keys.dtype),
            pltpu.VMEM(values.shape, values.dtype),
            pltpu.SemaphoreType.DMA((3,)),
        ],
        compiler_params=pltpu.CompilerParams(vmem_limit_bytes=16 << 20),
        cost_estimate=pl.CostEstimate(flops=10**10, bytes_accessed=10**7, transcendentals=0),
        name="prep",
    )(positions, keys, values)


def piece_starts(rows, parts):
    piece = rows // parts
    me = lax.axis_index("heads")
    return piece, [pl.multiple_of((me ^ k) * piece, piece) for k in range(parts)]


def values_of(blocks):
    tiles = [b[t : t + HD, HD:] for b in blocks for t in range(0, b.shape[0], HD)]
    values_t = jnp.concatenate(tiles, axis=1)
    return jnp.concatenate([values_t, jnp.ones((ONES, values_t.shape[1]), jnp.bfloat16)], axis=0)


def attend(state, blocks, allowed=None):
    queries_ref, shift_ref, total_ref, acc_ref = state
    width = queries_ref.shape[1]
    tile = min(TILE, width)

    def step(i, carry):
        cols = pl.ds(pl.multiple_of(i * tile, tile), tile)
        keys = [b[:, :HD] for b in blocks]
        keys = keys[0] if len(keys) == 1 else jnp.concatenate(keys, axis=0)
        s = jnp.dot(keys, queries_ref[:, cols], preferred_element_type=jnp.float32)
        if allowed is not None:
            s = jnp.where(jnp.concatenate([allowed] * (tile // allowed.shape[1]), 1), s, NEG_FILL)
        p = jnp.exp2(s * EXP2_SCALE - shift_ref[:, cols]).astype(jnp.bfloat16)
        mixed = jnp.dot(values_of(blocks), p, preferred_element_type=jnp.float32)
        if allowed is None:
            total_ref[:, cols] += mixed[HD : HD + 1]
            acc_ref[:, cols] += mixed[:HD]
        else:
            total_ref[:, cols] = mixed[HD : HD + 1]
            acc_ref[:, cols] = mixed[:HD]
        return carry

    lax.fori_loop(0, width // tile, step, 0)


def first_kernel(heads, group, parts, q_ref, table_ref, *refs):
    own_refs, out_refs = refs[:heads], refs[heads:]
    rows = q_ref.shape[0]
    piece, starts = piece_starts(rows, parts)
    table = jnp.concatenate([table_ref[pl.ds(s, piece), :] for s in starts], axis=0)
    lane = lax.broadcasted_iota(jnp.int32, (1, piece), 1)
    row_index = jnp.concatenate([lane + s for s in starts], axis=1)
    allowed = lax.broadcasted_iota(jnp.int32, (rows, rows), 0) <= row_index
    for head, own_ref in enumerate(own_refs):
        state = out_refs[4 * head : 4 * head + 4]
        queries_ref, shift_ref = state[:2]
        own_t = jnp.concatenate([own_ref[pl.ds(s, piece), :HD] for s in starts], axis=0)
        own_t = own_t.astype(jnp.float32).T
        for g in range(group):
            cols = slice((head * group + g) * HD, (head * group + g + 1) * HD)
            x = jnp.concatenate([q_ref[pl.ds(s, piece), cols] for s in starts], axis=0)
            x = rotate(x.astype(jnp.float32), table[:, :HD], table[:, HD:])
            x = x.T.astype(jnp.bfloat16)
            out = slice(g * rows, (g + 1) * rows)
            queries_ref[:, out] = x
            own_score = jnp.sum(x.astype(jnp.float32) * own_t, axis=0, keepdims=True)
            shift_ref[:, out] = own_score * EXP2_SCALE
        attend(state, [own_ref], allowed)


def attend_first(queries, table, owns, group, parts):
    rows = queries.shape[0]
    width = group * rows
    vmem = pl.BlockSpec(memory_space=pltpu.VMEM)
    flat = pl.pallas_call(
        functools.partial(first_kernel, len(owns), group, parts),
        in_specs=[vmem] * (2 + len(owns)),
        out_specs=[vmem] * (4 * len(owns)),
        out_shape=[
            jax.ShapeDtypeStruct((HD, width), jnp.bfloat16),
            jax.ShapeDtypeStruct((1, width), jnp.float32),
            jax.ShapeDtypeStruct((1, width), jnp.float32),
            jax.ShapeDtypeStruct((HD, width), jnp.float32),
        ]
        * len(owns),
        compiler_params=pltpu.CompilerParams(vmem_limit_bytes=LIMIT),
        cost_estimate=cost(width * len(owns), rows),
        name="attend_first",
    )(queries, table, *owns)
    return [tuple(flat[4 * h : 4 * h + 4]) for h in range(len(owns))]


def cost(width, keys):
    return pl.CostEstimate(flops=8 * width * keys * HD, bytes_accessed=0, transcendentals=0)


def attend_groups(groups, refs, state):
    rank = lax.axis_index("ctx")
    chip, core = rank // 2, rank % 2
    refs = list(refs)
    for step in groups:
        blocks = [refs.pop(0) for _ in range(1 if step == 0 else 2)]
        there = core == 1 if step == 0 else chip >= step
        pl.when(there)(functools.partial(attend, state, blocks))


def next_kernel(groups, queries_ref, shift_ref, total_in, acc_in, *refs):
    del total_in, acc_in
    attend_groups(groups, refs[:-2], (queries_ref, shift_ref, refs[-2], refs[-1]))


def attend_next(state, groups, blocks):
    queries, shift, total, acc = state
    vmem = pl.BlockSpec(memory_space=pltpu.VMEM)
    total, acc = pl.pallas_call(
        functools.partial(next_kernel, groups),
        in_specs=[vmem] * (4 + len(blocks)),
        out_specs=[vmem] * 2,
        out_shape=[jax.ShapeDtypeStruct(x.shape, x.dtype) for x in (total, acc)],
        input_output_aliases={2: 0, 3: 1},
        compiler_params=pltpu.CompilerParams(vmem_limit_bytes=LIMIT),
        cost_estimate=cost(queries.shape[1], sum(b.shape[0] for b in blocks)),
        name="attend_next",
    )(queries, shift, total, acc, *blocks)
    return queries, shift, total, acc


def recompute(rows, parts, queries_ref, every, total_ref, acc_ref, top_ref, blocks_ref, sems):
    rank = lax.axis_index("ctx")
    chip, core = rank // 2, rank % 2
    piece, starts = piece_starts(rows, parts)
    lane = lax.broadcasted_iota(jnp.int32, (1, piece), 1)
    row_index = jnp.concatenate([lane + s for s in starts], axis=1)
    key_index = lax.broadcasted_iota(jnp.int32, (rows, rows), 0)
    width = queries_ref.shape[1]
    copies = [
        pltpu.make_async_copy(ref, blocks_ref.at[pl.ds(b * rows, rows)], sems.at[b])
        for b, ref in enumerate(every)
    ]
    for copy in copies:
        copy.start()
    top_ref[...] = jnp.full(top_ref.shape, NEG_FILL, jnp.float32)
    total_ref[...] = jnp.zeros(total_ref.shape, jnp.float32)
    acc_ref[...] = jnp.zeros(acc_ref.shape, jnp.float32)
    for copy in copies:
        copy.wait()

    def block_step(b, carry):
        valid = jnp.where(b == 1, core == 1, chip >= b // 2)
        ahead = jnp.where(b == 0, 0, rows)
        block_ref = blocks_ref.at[pl.ds(pl.multiple_of(b * rows, rows), rows)]

        def tile_step(t, carry):
            cols = pl.ds(pl.multiple_of(t * rows, rows), rows)
            s = jnp.dot(block_ref[:, :HD], queries_ref[:, cols], preferred_element_type=jnp.float32)
            s = jnp.where(key_index - ahead <= row_index, s, NEG_FILL)
            top = jnp.maximum(top_ref[:, cols], jnp.max(s, axis=0, keepdims=True))
            p = jnp.exp2((s - top) * EXP2_SCALE)
            factor = jnp.exp2((top_ref[:, cols] - top) * EXP2_SCALE)
            mixed = jnp.dot(
                values_of([block_ref]), p.astype(jnp.bfloat16), preferred_element_type=jnp.float32
            )
            total_ref[:, cols] = total_ref[:, cols] * factor + mixed[HD : HD + 1]
            acc_ref[:, cols] = acc_ref[:, cols] * factor + mixed[:HD]
            top_ref[:, cols] = top
            return carry

        @pl.when(valid)
        def _():
            lax.fori_loop(0, width // rows, tile_step, 0)

        return carry

    lax.fori_loop(0, len(every), block_step, 0)


def last_kernel(groups, count, every_count, rows, parts, queries_ref, shift_ref, total_in, acc_in, *refs):
    refs = list(refs)
    blocks, refs = refs[:count], refs[count:]
    every, refs = refs[:every_count], refs[every_count:]
    out_refs, (total_ref, acc_ref, top_ref, blocks_ref, sems) = refs[:parts], refs[parts:]
    total_ref[...] = total_in[...]
    acc_ref[...] = acc_in[...]
    attend_groups(groups, blocks, (queries_ref, shift_ref, total_ref, acc_ref))
    in_range = jnp.max(total_ref[...]) <= TOTAL_LIMIT

    @pl.when(jnp.logical_not(in_range))
    def _():
        recompute(rows, parts, queries_ref, every, total_ref, acc_ref, top_ref, blocks_ref, sems)

    piece = rows // parts

    def finish(g, carry):
        cols = pl.ds(pl.multiple_of(g * rows, rows), rows)
        out = pl.ds(pl.multiple_of(g * HD, HD), HD)
        result = (acc_ref[:, cols] * (1.0 / total_ref[:, cols])).T.astype(jnp.bfloat16)
        for k in range(parts):
            out_refs[k][:, out] = result[k * piece : (k + 1) * piece]
        return carry

    lax.fori_loop(0, queries_ref.shape[1] // rows, finish, 0, unroll=True)


def attend_last(state, groups, blocks, every, parts):
    queries, shift, total, acc = state
    rows = every[0].shape[0]
    group = queries.shape[1] // rows
    vmem, anywhere = pl.BlockSpec(memory_space=pltpu.VMEM), pl.BlockSpec(memory_space=pl.ANY)
    return pl.pallas_call(
        functools.partial(last_kernel, groups, len(blocks), len(every), rows, parts),
        in_specs=[vmem] * (4 + len(blocks)) + [anywhere] * len(every),
        out_specs=[vmem] * parts,
        out_shape=[jax.ShapeDtypeStruct((rows // parts, group * HD), jnp.bfloat16)] * parts,
        scratch_shapes=[
            pltpu.VMEM(total.shape, jnp.float32),
            pltpu.VMEM(acc.shape, jnp.float32),
            pltpu.VMEM(total.shape, jnp.float32),
            pltpu.VMEM((len(every) * rows, 2 * HD), jnp.bfloat16),
            pltpu.SemaphoreType.DMA((len(every),)),
        ],
        compiler_params=pltpu.CompilerParams(vmem_limit_bytes=LIMIT),
        cost_estimate=cost(queries.shape[1], sum(b.shape[0] for b in blocks)),
        name="attend_last",
    )(queries, shift, total, acc, *blocks, *every)


def place_kernel(heads, parts, *refs):
    pieces, out_ref, sems = refs[: heads * parts], refs[-2], refs[-1]
    me = lax.axis_index("heads")
    copies = []
    for head in range(heads):
        for k in range(parts):
            src = pieces[head * parts + k]
            cols = src.shape[1]
            start = pl.multiple_of(((me ^ k) * heads + head) * cols, cols)
            copies.append(
                pltpu.make_async_copy(src, out_ref.at[:, pl.ds(start, cols)], sems.at[len(copies)])
            )
    for c in copies:
        c.start()
    for c in copies:
        c.wait()


def place(pieces, heads, parts):
    rows, cols = pieces[0].shape
    return pl.pallas_call(
        functools.partial(place_kernel, heads, parts),
        in_specs=[pl.BlockSpec(memory_space=pltpu.VMEM)] * len(pieces),
        out_specs=pl.BlockSpec(memory_space=pl.ANY),
        out_shape=jax.ShapeDtypeStruct((rows, cols * len(pieces)), jnp.bfloat16),
        compiler_params=pltpu.CompilerParams(vmem_limit_bytes=16 << 20),
        scratch_shapes=[pltpu.SemaphoreType.DMA((len(pieces),))],
        name="place",
    )(*pieces)


def after(value, *earlier):
    return lax.optimization_barrier((value, *earlier))[0]


def local(ctx_size, parts, queries, keys, values, positions):
    kv_heads = keys.shape[1] // HD
    group = queries.shape[1] // (kv_heads * HD)
    chips = ctx_size // 2
    heads = range(kv_heads)
    swap = [(c, c ^ 1) for c in range(ctx_size)]

    def upward(step, cross=0):
        low = 2 * (step - 1)
        top = [(c, (c + 2 if c + 2 < ctx_size else low + c % 2) ^ cross) for c in range(low, ctx_size)]
        return swap[:low] + top

    direct = chips > 3 and kv_heads > 1

    table, *packs = prep(keys, values, positions)
    near = [[pack, lax.ppermute(pack, "ctx", upward(1))] for pack in packs]
    far = [[lax.ppermute(pack, "ctx", swap)] for pack in packs]
    states = attend_first(queries, table, packs, group, parts)
    latest = [states[-1][2], *(far[h][0] for h in heads)]

    def pass_on(head, step, *earlier):
        block = after(near[head][step], *earlier)
        near[head][step] = block
        if step + 1 == chips - 1 and direct and head == kv_heads - 1:
            near[head].append(lax.ppermute(block, "ctx", upward(step + 1)))
            far[head].append(lax.ppermute(block, "ctx", swap))
            far[head].append(lax.ppermute(block, "ctx", upward(step + 1, 1)))
            return
        if step + 1 < chips:
            near[head].append(lax.ppermute(block, "ctx", upward(step + 1)))
        if len(far[head]) == step:
            far[head].append(lax.ppermute(block, "ctx", swap))

    def blocks_of(head, steps):
        out = []
        for s in steps:
            out += [far[head][0]] if s == 0 else [near[head][s], far[head][s]]
        return out

    def state_after(head, earlier):
        queries_t, shift, total, acc = states[head]
        return queries_t, shift, after(total, *earlier), acc

    order = [(0, [0, 1])] + [(0, [s]) for s in range(2, chips - 1)]
    for head in range(1, kv_heads):
        order += [(head, [0, 1])] + [(head, [s]) for s in range(2, chips - 2)]
    done = [0] * kv_heads
    pass_on(0, 1, *latest)
    latest = latest[:1] + [near[h][1] for h in heads]
    for i, (head, steps) in enumerate(order):
        states[head] = attend_next(state_after(head, latest), steps, blocks_of(head, steps))
        done[head] = steps[-1]
        latest = [states[head][2]]
        if done[head] + 1 < chips and (head == kv_heads - 1 or done[head] + 1 < chips - 1):
            pass_on(head, done[head] + 1, *latest)
            latest.append(far[head][done[head] + 1])
        elif head < kv_heads - 1:
            pass_on(head + 1, 1, *latest)
            pass_on(head, chips - 1, *latest)
            latest.append(far[head + 1][1])
    pieces = []
    sent = []
    for head in heads:
        if chips - done[head] > 2:
            steps = list(range(done[head] + 1, chips - 1))
            states[head] = attend_next(state_after(head, latest), steps, blocks_of(head, steps))
            done[head], latest = chips - 2, [states[head][2]]
        steps = list(range(done[head] + 1, chips))
        outs = attend_last(
            state_after(head, latest),
            steps,
            blocks_of(head, steps),
            [b for pair in zip(near[head], far[head], strict=True) for b in pair],
            parts,
        )
        latest = [outs[0]]
        out = [after(outs[k], *sent) if k else outs[k] for k in range(parts)]
        out[1:] = [lax.ppermute(out[k], "heads", [(i, i ^ k) for i in range(parts)]) for k in range(1, parts)]
        sent = out[1:2]
        pieces += out
    return place(pieces, kv_heads, parts)


def solution(mesh):
    return jax.shard_map(
        functools.partial(local, mesh.shape["ctx"], mesh.shape["heads"]),
        mesh=mesh,
        in_specs=(P("ctx", "heads"), P("ctx", "heads"), P("ctx", "heads"), P("ctx")),
        out_specs=P(("ctx", "heads"), None),
        check_vma=False,
    )
```

```python
import functools
import math

import jax
import jax.numpy as jnp
import numpy as np
from jax import lax
from jax.experimental import pallas as pl
from jax.experimental.pallas import tpu as pltpu
from jax.sharding import PartitionSpec as P

HD = 128
HALF = HD // 2
NEG_FILL = -1e30
EXP2_SCALE = math.log2(math.e) / math.sqrt(HD)
TOTAL_LIMIT = 2.0**100
TILE = 1536
ONES = 16
LIMIT = 24 << 20


def inverse_frequencies():
    base = 500000.0 ** (-2.0 * np.arange(HALF) / HD)
    wave = 2.0 * math.pi / base
    blend = (8192.0 / wave - 1.0) / 3.0
    middle = (1.0 - blend) * base / 8.0 + blend * base
    return np.where(wave < 2048.0, base, np.where(wave > 8192.0, base / 8.0, middle)).astype(np.float32)


def frequency_row():
    lane = lax.broadcasted_iota(jnp.int32, (1, HD), 1) % HALF
    row = jnp.zeros((1, HD), jnp.float32)
    for i, freq in enumerate(inverse_frequencies()):
        row = jnp.where(lane == i, float(freq), row)
    return row


def cos_sin(angle):
    turns = jnp.round(angle * (2.0 / math.pi))
    rest = angle - turns * 1.5703125
    rest = rest - turns * 4.837512969970703e-4
    rest = rest - turns * 7.54978995489188e-8
    quadrant = turns.astype(jnp.int32) & 3
    sq = rest * rest
    sine = rest + rest * sq * (-1.6666654611e-1 + sq * (8.3321608736e-3 - sq * 1.9515295891e-4))
    cosine = (
        1.0
        - 0.5 * sq
        + sq * sq * (4.166664568298827e-2 + sq * (-1.388731625493765e-3 + sq * 2.443315711809948e-5))
    )
    odd = (quadrant & 1) == 1
    cos_out = jnp.where(odd, sine, cosine)
    sin_out = jnp.where(odd, cosine, sine)
    cos_out = jnp.where((quadrant == 1) | (quadrant == 2), -cos_out, cos_out)
    sin_out = jnp.where(quadrant >= 2, -sin_out, sin_out)
    return cos_out, sin_out


def rotate(x, cosine, sine):
    return x * cosine + pltpu.roll(x, HALF, 1) * sine


def table_kernel(pos_ref, table_ref):
    sign = jnp.where(lax.broadcasted_iota(jnp.int32, (HD, HD), 1) < HALF, -1.0, 1.0)
    freq = frequency_row()
    for at in range(0, pos_ref.shape[0], HD):
        rows = slice(at, at + HD)
        pos = pos_ref[rows].reshape(1, HD).astype(jnp.float32)
        pos = jnp.broadcast_to(pos, (HD, HD)).T
        cosine, sine = cos_sin(pos * freq)
        table_ref[rows, :HD] = cosine
        table_ref[rows, HD:] = sine * sign


def pack_kernel(heads, table_ref, k_ref, v_ref, *pack_refs):
    for at in range(0, k_ref.shape[0], HD):
        rows = slice(at, at + HD)
        for head in range(heads):
            cols = slice(head * HD, (head + 1) * HD)
            key = rotate(k_ref[rows, cols].astype(jnp.float32), table_ref[rows, :HD], table_ref[rows, HD:])
            pack_refs[head][rows, :HD] = key.astype(jnp.bfloat16)
            pack_refs[head][rows, HD:] = v_ref[rows, cols].T


def prep(keys, values, positions):
    rows, cols = keys.shape
    heads = cols // HD
    vmem = pl.BlockSpec(memory_space=pltpu.VMEM)
    params = pltpu.CompilerParams(vmem_limit_bytes=16 << 20)
    table = pl.pallas_call(
        table_kernel,
        in_specs=[vmem],
        out_specs=vmem,
        out_shape=jax.ShapeDtypeStruct((rows, 2 * HD), jnp.float32),
        compiler_params=params,
        cost_estimate=pl.CostEstimate(flops=10**10, bytes_accessed=0, transcendentals=0),
        name="table",
    )(positions)
    packs = pl.pallas_call(
        functools.partial(pack_kernel, heads),
        in_specs=[vmem] * 3,
        out_specs=[vmem] * heads,
        out_shape=[jax.ShapeDtypeStruct((rows, 2 * HD), jnp.bfloat16)] * heads,
        compiler_params=params,
        name="pack",
    )(table, keys, values)
    return table, *packs


def piece_starts(rows, parts):
    piece = rows // parts
    me = lax.axis_index("heads")
    return piece, [pl.multiple_of((me ^ k) * piece, piece) for k in range(parts)]


def values_of(blocks):
    tiles = [b[t : t + HD, HD:] for b in blocks for t in range(0, b.shape[0], HD)]
    values_t = jnp.concatenate(tiles, axis=1)
    return jnp.concatenate([values_t, jnp.ones((ONES, values_t.shape[1]), jnp.bfloat16)], axis=0)


def attend(state, blocks, allowed=None):
    queries_ref, shift_ref, total_ref, acc_ref = state
    width = queries_ref.shape[1]
    tile = min(TILE, width)

    def step(i, carry):
        cols = pl.ds(pl.multiple_of(i * tile, tile), tile)
        keys = [b[:, :HD] for b in blocks]
        keys = keys[0] if len(keys) == 1 else jnp.concatenate(keys, axis=0)
        s = jnp.dot(keys, queries_ref[:, cols], preferred_element_type=jnp.float32)
        if allowed is not None:
            s = jnp.where(jnp.concatenate([allowed] * (tile // allowed.shape[1]), 1), s, NEG_FILL)
        p = jnp.exp2(s * EXP2_SCALE - shift_ref[:, cols]).astype(jnp.bfloat16)
        mixed = jnp.dot(values_of(blocks), p, preferred_element_type=jnp.float32)
        if allowed is None:
            total_ref[:, cols] += mixed[HD : HD + 1]
            acc_ref[:, cols] += mixed[:HD]
        else:
            total_ref[:, cols] = mixed[HD : HD + 1]
            acc_ref[:, cols] = mixed[:HD]
        return carry

    lax.fori_loop(0, width // tile, step, 0)


def first_kernel(heads, group, parts, q_ref, table_ref, *refs):
    own_refs, out_refs = refs[:heads], refs[heads:]
    rows = q_ref.shape[0]
    piece, starts = piece_starts(rows, parts)
    table = jnp.concatenate([table_ref[pl.ds(s, piece), :] for s in starts], axis=0)
    lane = lax.broadcasted_iota(jnp.int32, (1, piece), 1)
    row_index = jnp.concatenate([lane + s for s in starts], axis=1)
    allowed = lax.broadcasted_iota(jnp.int32, (rows, rows), 0) <= row_index
    for head, own_ref in enumerate(own_refs):
        state = out_refs[4 * head : 4 * head + 4]
        queries_ref, shift_ref = state[:2]
        own_t = jnp.concatenate([own_ref[pl.ds(s, piece), :HD] for s in starts], axis=0)
        own_t = own_t.astype(jnp.float32).T
        for g in range(group):
            cols = slice((head * group + g) * HD, (head * group + g + 1) * HD)
            x = jnp.concatenate([q_ref[pl.ds(s, piece), cols] for s in starts], axis=0)
            x = rotate(x.astype(jnp.float32), table[:, :HD], table[:, HD:])
            x = x.T.astype(jnp.bfloat16)
            out = slice(g * rows, (g + 1) * rows)
            queries_ref[:, out] = x
            own_score = jnp.sum(x.astype(jnp.float32) * own_t, axis=0, keepdims=True)
            shift_ref[:, out] = own_score * EXP2_SCALE
        attend(state, [own_ref], allowed)


def attend_first(queries, table, owns, group, parts):
    rows = queries.shape[0]
    width = group * rows
    vmem = pl.BlockSpec(memory_space=pltpu.VMEM)
    flat = pl.pallas_call(
        functools.partial(first_kernel, len(owns), group, parts),
        in_specs=[vmem] * (2 + len(owns)),
        out_specs=[vmem] * (4 * len(owns)),
        out_shape=[
            jax.ShapeDtypeStruct((HD, width), jnp.bfloat16),
            jax.ShapeDtypeStruct((1, width), jnp.float32),
            jax.ShapeDtypeStruct((1, width), jnp.float32),
            jax.ShapeDtypeStruct((HD, width), jnp.float32),
        ]
        * len(owns),
        compiler_params=pltpu.CompilerParams(vmem_limit_bytes=LIMIT),
        cost_estimate=cost(width * len(owns), rows),
        name="attend_first",
    )(queries, table, *owns)
    return [tuple(flat[4 * h : 4 * h + 4]) for h in range(len(owns))]


def cost(width, keys):
    return pl.CostEstimate(flops=8 * width * keys * HD, bytes_accessed=0, transcendentals=0)


def attend_groups(groups, refs, state):
    rank = lax.axis_index("ctx")
    chip, core = rank // 2, rank % 2
    refs = list(refs)
    for step in groups:
        blocks = [refs.pop(0) for _ in range(1 if step == 0 else 2)]
        there = core == 1 if step == 0 else chip >= step
        pl.when(there)(functools.partial(attend, state, blocks))


def next_kernel(groups, queries_ref, shift_ref, total_in, acc_in, *refs):
    del total_in, acc_in
    attend_groups(groups, refs[:-2], (queries_ref, shift_ref, refs[-2], refs[-1]))


def attend_next(state, groups, blocks):
    queries, shift, total, acc = state
    vmem = pl.BlockSpec(memory_space=pltpu.VMEM)
    total, acc = pl.pallas_call(
        functools.partial(next_kernel, groups),
        in_specs=[vmem] * (4 + len(blocks)),
        out_specs=[vmem] * 2,
        out_shape=[jax.ShapeDtypeStruct(x.shape, x.dtype) for x in (total, acc)],
        input_output_aliases={2: 0, 3: 1},
        compiler_params=pltpu.CompilerParams(vmem_limit_bytes=LIMIT),
        cost_estimate=cost(queries.shape[1], sum(b.shape[0] for b in blocks)),
        name="attend_next",
    )(queries, shift, total, acc, *blocks)
    return queries, shift, total, acc


def recompute(rows, parts, queries_ref, every, total_ref, acc_ref, top_ref, blocks_ref, sems):
    rank = lax.axis_index("ctx")
    chip, core = rank // 2, rank % 2
    piece, starts = piece_starts(rows, parts)
    lane = lax.broadcasted_iota(jnp.int32, (1, piece), 1)
    row_index = jnp.concatenate([lane + s for s in starts], axis=1)
    key_index = lax.broadcasted_iota(jnp.int32, (rows, rows), 0)
    width = queries_ref.shape[1]
    copies = [
        pltpu.make_async_copy(ref, blocks_ref.at[pl.ds(b * rows, rows)], sems.at[b])
        for b, ref in enumerate(every)
    ]
    for copy in copies:
        copy.start()
    top_ref[...] = jnp.full(top_ref.shape, NEG_FILL, jnp.float32)
    total_ref[...] = jnp.zeros(total_ref.shape, jnp.float32)
    acc_ref[...] = jnp.zeros(acc_ref.shape, jnp.float32)
    for copy in copies:
        copy.wait()

    def block_step(b, carry):
        valid = jnp.where(b == 1, core == 1, chip >= b // 2)
        ahead = jnp.where(b == 0, 0, rows)
        block_ref = blocks_ref.at[pl.ds(pl.multiple_of(b * rows, rows), rows)]

        def tile_step(t, carry):
            cols = pl.ds(pl.multiple_of(t * rows, rows), rows)
            s = jnp.dot(block_ref[:, :HD], queries_ref[:, cols], preferred_element_type=jnp.float32)
            s = jnp.where(key_index - ahead <= row_index, s, NEG_FILL)
            top = jnp.maximum(top_ref[:, cols], jnp.max(s, axis=0, keepdims=True))
            p = jnp.exp2((s - top) * EXP2_SCALE)
            factor = jnp.exp2((top_ref[:, cols] - top) * EXP2_SCALE)
            mixed = jnp.dot(
                values_of([block_ref]), p.astype(jnp.bfloat16), preferred_element_type=jnp.float32
            )
            total_ref[:, cols] = total_ref[:, cols] * factor + mixed[HD : HD + 1]
            acc_ref[:, cols] = acc_ref[:, cols] * factor + mixed[:HD]
            top_ref[:, cols] = top
            return carry

        @pl.when(valid)
        def _():
            lax.fori_loop(0, width // rows, tile_step, 0)

        return carry

    lax.fori_loop(0, len(every), block_step, 0)


def last_kernel(groups, count, every_count, rows, parts, queries_ref, shift_ref, total_in, acc_in, *refs):
    refs = list(refs)
    blocks, refs = refs[:count], refs[count:]
    every, refs = refs[:every_count], refs[every_count:]
    out_refs, (total_ref, acc_ref, top_ref, blocks_ref, sems) = refs[:parts], refs[parts:]
    total_ref[...] = total_in[...]
    acc_ref[...] = acc_in[...]
    attend_groups(groups, blocks, (queries_ref, shift_ref, total_ref, acc_ref))
    in_range = jnp.max(total_ref[...]) <= TOTAL_LIMIT

    @pl.when(jnp.logical_not(in_range))
    def _():
        recompute(rows, parts, queries_ref, every, total_ref, acc_ref, top_ref, blocks_ref, sems)

    piece = rows // parts

    def finish(g, carry):
        cols = pl.ds(pl.multiple_of(g * rows, rows), rows)
        out = pl.ds(pl.multiple_of(g * HD, HD), HD)
        result = (acc_ref[:, cols] * (1.0 / total_ref[:, cols])).astype(jnp.bfloat16).T
        for k in range(parts):
            out_refs[k][:, out] = result[k * piece : (k + 1) * piece]
        return carry

    lax.fori_loop(0, queries_ref.shape[1] // rows, finish, 0, unroll=True)


def attend_last(state, groups, blocks, every, parts):
    queries, shift, total, acc = state
    rows = every[0].shape[0]
    group = queries.shape[1] // rows
    vmem, anywhere = pl.BlockSpec(memory_space=pltpu.VMEM), pl.BlockSpec(memory_space=pl.ANY)
    return pl.pallas_call(
        functools.partial(last_kernel, groups, len(blocks), len(every), rows, parts),
        in_specs=[vmem] * (4 + len(blocks)) + [anywhere] * len(every),
        out_specs=[vmem] * parts,
        out_shape=[jax.ShapeDtypeStruct((rows // parts, group * HD), jnp.bfloat16)] * parts,
        scratch_shapes=[
            pltpu.VMEM(total.shape, jnp.float32),
            pltpu.VMEM(acc.shape, jnp.float32),
            pltpu.VMEM(total.shape, jnp.float32),
            pltpu.VMEM((len(every) * rows, 2 * HD), jnp.bfloat16),
            pltpu.SemaphoreType.DMA((len(every),)),
        ],
        compiler_params=pltpu.CompilerParams(vmem_limit_bytes=LIMIT),
        cost_estimate=cost(queries.shape[1], sum(b.shape[0] for b in blocks)),
        name="attend_last",
    )(queries, shift, total, acc, *blocks, *every)


def place_kernel(heads, parts, *refs):
    pieces, out_ref, sems = refs[: heads * parts], refs[-2], refs[-1]
    me = lax.axis_index("heads")
    copies = []
    for head in range(heads):
        for k in range(parts):
            src = pieces[head * parts + k]
            cols = src.shape[1]
            start = pl.multiple_of(((me ^ k) * heads + head) * cols, cols)
            copies.append(
                pltpu.make_async_copy(src, out_ref.at[:, pl.ds(start, cols)], sems.at[len(copies)])
            )
    for c in copies:
        c.start()
    for c in copies:
        c.wait()


def place(pieces, heads, parts):
    rows, cols = pieces[0].shape
    return pl.pallas_call(
        functools.partial(place_kernel, heads, parts),
        in_specs=[pl.BlockSpec(memory_space=pltpu.VMEM)] * len(pieces),
        out_specs=pl.BlockSpec(memory_space=pl.ANY),
        out_shape=jax.ShapeDtypeStruct((rows, cols * len(pieces)), jnp.bfloat16),
        compiler_params=pltpu.CompilerParams(vmem_limit_bytes=16 << 20),
        scratch_shapes=[pltpu.SemaphoreType.DMA((len(pieces),))],
        name="place",
    )(*pieces)


def after(value, *earlier):
    return lax.optimization_barrier((value, *earlier))[0]


def local(ctx_size, parts, queries, keys, values, positions):
    kv_heads = keys.shape[1] // HD
    group = queries.shape[1] // (kv_heads * HD)
    chips = ctx_size // 2
    heads = range(kv_heads)
    swap = [(c, c ^ 1) for c in range(ctx_size)]

    def upward(step, cross=0):
        low = 2 * (step - 1)
        top = [(c, (c + 2 if c + 2 < ctx_size else low + c % 2) ^ cross) for c in range(low, ctx_size)]
        return swap[:low] + top

    direct = chips > 3 and kv_heads > 1

    table, *packs = prep(keys, values, positions)
    near = [[pack, lax.ppermute(pack, "ctx", upward(1))] for pack in packs]
    far = [[lax.ppermute(pack, "ctx", swap)] for pack in packs]
    states = attend_first(queries, table, packs, group, parts)
    latest = [states[-1][2], *(far[h][0] for h in heads)]

    def pass_on(head, step, *earlier):
        block = after(near[head][step], *earlier)
        near[head][step] = block
        if step + 1 == chips - 1 and direct and head == kv_heads - 1:
            near[head].append(lax.ppermute(block, "ctx", upward(step + 1)))
            far[head].append(lax.ppermute(block, "ctx", swap))
            far[head].append(lax.ppermute(block, "ctx", upward(step + 1, 1)))
            return
        if step + 1 < chips:
            near[head].append(lax.ppermute(block, "ctx", upward(step + 1)))
        if len(far[head]) == step:
            far[head].append(lax.ppermute(block, "ctx", swap))

    def blocks_of(head, steps):
        out = []
        for s in steps:
            out += [far[head][0]] if s == 0 else [near[head][s], far[head][s]]
        return out

    def state_after(head, earlier):
        queries_t, shift, total, acc = states[head]
        return queries_t, shift, after(total, *earlier), acc

    order = [(0, [0, 1])] + [(0, [s]) for s in range(2, chips - 1)]
    for head in range(1, kv_heads):
        order += [(head, [0, 1])] + [(head, [s]) for s in range(2, chips - 2)]
    done = [0] * kv_heads
    pass_on(0, 1, *latest)
    latest = latest[:1] + [near[h][1] for h in heads]
    for i, (head, steps) in enumerate(order):
        states[head] = attend_next(state_after(head, latest), steps, blocks_of(head, steps))
        done[head] = steps[-1]
        latest = [states[head][2]]
        if done[head] + 1 < chips and (head == kv_heads - 1 or done[head] + 1 < chips - 1):
            pass_on(head, done[head] + 1, *latest)
            latest.append(far[head][done[head] + 1])
        elif head < kv_heads - 1:
            pass_on(head + 1, 1, *latest)
            pass_on(head, chips - 1, *latest)
            latest.append(far[head + 1][1])
    pieces = []
    sent = []
    for head in heads:
        if chips - done[head] > 2:
            steps = list(range(done[head] + 1, chips - 1))
            states[head] = attend_next(state_after(head, latest), steps, blocks_of(head, steps))
            done[head], latest = chips - 2, [states[head][2]]
        steps = list(range(done[head] + 1, chips))
        outs = attend_last(
            state_after(head, latest),
            steps,
            blocks_of(head, steps),
            [b for pair in zip(near[head], far[head], strict=True) for b in pair],
            parts,
        )
        latest = [outs[0]]
        out = [after(outs[k], *sent) if k else outs[k] for k in range(parts)]
        out[1:] = [lax.ppermute(out[k], "heads", [(i, i ^ k) for i in range(parts)]) for k in range(1, parts)]
        sent = out[1:2]
        pieces += out
    return place(pieces, kv_heads, parts)


def solution(mesh):
    return jax.shard_map(
        functools.partial(local, mesh.shape["ctx"], mesh.shape["heads"]),
        mesh=mesh,
        in_specs=(P("ctx", "heads"), P("ctx", "heads"), P("ctx", "heads"), P("ctx")),
        out_specs=P(("ctx", "heads"), None),
        check_vma=False,
    )
```

```python
import functools
import math

import jax
import jax.numpy as jnp
import numpy as np
from jax import lax
from jax.experimental import pallas as pl
from jax.experimental.pallas import tpu as pltpu
from jax.sharding import PartitionSpec as P

HD = 128
HALF = HD // 2
NEG_FILL = -1e30
EXP2_SCALE = math.log2(math.e) / math.sqrt(HD)
TOTAL_LIMIT = 2.0**100
TILE = 1536
ONES = 16
LIMIT = 24 << 20
MORE = 16


def inverse_frequencies():
    base = 500000.0 ** (-2.0 * np.arange(HALF) / HD)
    wave = 2.0 * math.pi / base
    blend = (8192.0 / wave - 1.0) / 3.0
    middle = (1.0 - blend) * base / 8.0 + blend * base
    return np.where(wave < 2048.0, base, np.where(wave > 8192.0, base / 8.0, middle)).astype(np.float32)


def frequency_row():
    lane = lax.broadcasted_iota(jnp.int32, (1, HD), 1) % HALF
    row = jnp.zeros((1, HD), jnp.float32)
    for i, freq in enumerate(inverse_frequencies()):
        row = jnp.where(lane == i, float(freq), row)
    return row


def cos_sin(angle):
    turns = jnp.round(angle * (2.0 / math.pi))
    rest = angle - turns * 1.5703125
    rest = rest - turns * 4.837512969970703e-4
    rest = rest - turns * 7.54978995489188e-8
    quadrant = turns.astype(jnp.int32) & 3
    sq = rest * rest
    sine = rest + rest * sq * (-1.6666654611e-1 + sq * (8.3321608736e-3 - sq * 1.9515295891e-4))
    cosine = (
        1.0
        - 0.5 * sq
        + sq * sq * (4.166664568298827e-2 + sq * (-1.388731625493765e-3 + sq * 2.443315711809948e-5))
    )
    odd = (quadrant & 1) == 1
    cos_out = jnp.where(odd, sine, cosine)
    sin_out = jnp.where(odd, cosine, sine)
    cos_out = jnp.where((quadrant == 1) | (quadrant == 2), -cos_out, cos_out)
    sin_out = jnp.where(quadrant >= 2, -sin_out, sin_out)
    return cos_out, sin_out


def rotate(x, cosine, sine):
    return x * cosine + pltpu.roll(x, HALF, 1) * sine


def table_kernel(pos_ref, table_ref):
    sign = jnp.where(lax.broadcasted_iota(jnp.int32, (HD, HD), 1) < HALF, -1.0, 1.0)
    freq = frequency_row()
    for at in range(0, pos_ref.shape[0], HD):
        rows = slice(at, at + HD)
        pos = pos_ref[rows].reshape(1, HD).astype(jnp.float32)
        pos = jnp.broadcast_to(pos, (HD, HD)).T
        cosine, sine = cos_sin(pos * freq)
        table_ref[rows, :HD] = cosine
        table_ref[rows, HD:] = sine * sign


def pack_kernel(heads, table_ref, k_ref, v_ref, *pack_refs):
    for at in range(0, k_ref.shape[0], HD):
        rows = slice(at, at + HD)
        for head in range(heads):
            cols = slice(head * HD, (head + 1) * HD)
            key = rotate(k_ref[rows, cols].astype(jnp.float32), table_ref[rows, :HD], table_ref[rows, HD:])
            pack_refs[head][rows, :HD] = key.astype(jnp.bfloat16)
            pack_refs[head][rows, HD:] = v_ref[rows, cols].T
    for pack_ref in pack_refs:
        if pack_ref.shape[0] > k_ref.shape[0]:
            more = slice(k_ref.shape[0], pack_ref.shape[0])
            pack_ref[more, :] = jnp.zeros((more.stop - more.start, 2 * HD), jnp.bfloat16)


def prep(keys, values, positions, extra):
    rows, cols = keys.shape
    heads = cols // HD
    vmem = pl.BlockSpec(memory_space=pltpu.VMEM)
    params = pltpu.CompilerParams(vmem_limit_bytes=16 << 20)
    table = pl.pallas_call(
        table_kernel,
        in_specs=[vmem],
        out_specs=vmem,
        out_shape=jax.ShapeDtypeStruct((rows, 2 * HD), jnp.float32),
        compiler_params=params,
        cost_estimate=pl.CostEstimate(flops=10**10, bytes_accessed=0, transcendentals=0),
        name="table",
    )(positions)
    packs = pl.pallas_call(
        functools.partial(pack_kernel, heads),
        in_specs=[vmem] * 3,
        out_specs=[vmem] * heads,
        out_shape=[jax.ShapeDtypeStruct((rows + more, 2 * HD), jnp.bfloat16) for more in extra],
        compiler_params=params,
        name="pack",
    )(table, keys, values)
    return table, *packs


def piece_starts(rows, parts):
    piece = rows // parts
    me = lax.axis_index("heads")
    return piece, [pl.multiple_of((me ^ k) * piece, piece) for k in range(parts)]


def trim(refs, rows):
    return [ref.at[pl.ds(0, rows)] if ref.shape[0] > rows else ref for ref in refs]


def values_of(blocks):
    tiles = [b[t : t + HD, HD:] for b in blocks for t in range(0, b.shape[0], HD)]
    values_t = jnp.concatenate(tiles, axis=1)
    return jnp.concatenate([values_t, jnp.ones((ONES, values_t.shape[1]), jnp.bfloat16)], axis=0)


def attend(state, blocks, allowed=None):
    queries_ref, shift_ref, total_ref, acc_ref = state
    width = queries_ref.shape[1]
    tile = min(TILE, width)

    def step(i, carry):
        cols = pl.ds(pl.multiple_of(i * tile, tile), tile)
        keys = [b[:, :HD] for b in blocks]
        keys = keys[0] if len(keys) == 1 else jnp.concatenate(keys, axis=0)
        s = jnp.dot(keys, queries_ref[:, cols], preferred_element_type=jnp.float32)
        if allowed is not None:
            s = jnp.where(jnp.concatenate([allowed] * (tile // allowed.shape[1]), 1), s, NEG_FILL)
        p = jnp.exp2(s * EXP2_SCALE - shift_ref[:, cols]).astype(jnp.bfloat16)
        mixed = jnp.dot(values_of(blocks), p, preferred_element_type=jnp.float32)
        if allowed is None:
            total_ref[:, cols] += mixed[HD : HD + 1]
            acc_ref[:, cols] += mixed[:HD]
        else:
            total_ref[:, cols] = mixed[HD : HD + 1]
            acc_ref[:, cols] = mixed[:HD]
        return carry

    lax.fori_loop(0, width // tile, step, 0)


def first_kernel(heads, group, parts, q_ref, table_ref, *refs):
    rows = q_ref.shape[0]
    own_refs, out_refs = trim(refs[:heads], rows), refs[heads:]
    piece, starts = piece_starts(rows, parts)
    table = jnp.concatenate([table_ref[pl.ds(s, piece), :] for s in starts], axis=0)
    lane = lax.broadcasted_iota(jnp.int32, (1, piece), 1)
    row_index = jnp.concatenate([lane + s for s in starts], axis=1)
    allowed = lax.broadcasted_iota(jnp.int32, (rows, rows), 0) <= row_index
    for head, own_ref in enumerate(own_refs):
        state = out_refs[4 * head : 4 * head + 4]
        queries_ref, shift_ref = state[:2]
        own_t = jnp.concatenate([own_ref[pl.ds(s, piece), :HD] for s in starts], axis=0)
        own_t = own_t.astype(jnp.float32).T
        for g in range(group):
            cols = slice((head * group + g) * HD, (head * group + g + 1) * HD)
            x = jnp.concatenate([q_ref[pl.ds(s, piece), cols] for s in starts], axis=0)
            x = rotate(x.astype(jnp.float32), table[:, :HD], table[:, HD:])
            x = x.T.astype(jnp.bfloat16)
            out = slice(g * rows, (g + 1) * rows)
            queries_ref[:, out] = x
            own_score = jnp.sum(x.astype(jnp.float32) * own_t, axis=0, keepdims=True)
            shift_ref[:, out] = own_score * EXP2_SCALE
        attend(state, [own_ref], allowed)


def attend_first(queries, table, owns, group, parts):
    rows = queries.shape[0]
    width = group * rows
    vmem = pl.BlockSpec(memory_space=pltpu.VMEM)
    flat = pl.pallas_call(
        functools.partial(first_kernel, len(owns), group, parts),
        in_specs=[vmem] * (2 + len(owns)),
        out_specs=[vmem] * (4 * len(owns)),
        out_shape=[
            jax.ShapeDtypeStruct((HD, width), jnp.bfloat16),
            jax.ShapeDtypeStruct((1, width), jnp.float32),
            jax.ShapeDtypeStruct((1, width), jnp.float32),
            jax.ShapeDtypeStruct((HD, width), jnp.float32),
        ]
        * len(owns),
        compiler_params=pltpu.CompilerParams(vmem_limit_bytes=LIMIT),
        cost_estimate=cost(width * len(owns), rows),
        name="attend_first",
    )(queries, table, *owns)
    return [tuple(flat[4 * h : 4 * h + 4]) for h in range(len(owns))]


def cost(width, keys, share=1):
    return pl.CostEstimate(flops=share * 8 * width * keys * HD, bytes_accessed=0, transcendentals=0)


def attend_groups(groups, refs, state, rows):
    rank = lax.axis_index("ctx")
    chip, core = rank // 2, rank % 2
    refs = trim(refs, rows)
    for step in groups:
        blocks = [refs.pop(0) for _ in range(1 if step == 0 else 2)]
        there = core == 1 if step == 0 else chip >= step
        pl.when(there)(functools.partial(attend, state, blocks))


def next_kernel(groups, rows, queries_ref, shift_ref, total_in, acc_in, *refs):
    del total_in, acc_in
    attend_groups(groups, refs[:-2], (queries_ref, shift_ref, refs[-2], refs[-1]), rows)


def attend_next(state, groups, blocks, rows, share=1):
    queries, shift, total, acc = state
    vmem = pl.BlockSpec(memory_space=pltpu.VMEM)
    total, acc = pl.pallas_call(
        functools.partial(next_kernel, groups, rows),
        in_specs=[vmem] * (4 + len(blocks)),
        out_specs=[vmem] * 2,
        out_shape=[jax.ShapeDtypeStruct(x.shape, x.dtype) for x in (total, acc)],
        input_output_aliases={2: 0, 3: 1},
        compiler_params=pltpu.CompilerParams(vmem_limit_bytes=LIMIT),
        cost_estimate=cost(queries.shape[1], sum(b.shape[0] for b in blocks), share),
        name="attend_next",
    )(queries, shift, total, acc, *blocks)
    return queries, shift, total, acc


def recompute(rows, parts, queries_ref, every, total_ref, acc_ref, top_ref, blocks_ref, sems):
    rank = lax.axis_index("ctx")
    chip, core = rank // 2, rank % 2
    piece, starts = piece_starts(rows, parts)
    lane = lax.broadcasted_iota(jnp.int32, (1, piece), 1)
    row_index = jnp.concatenate([lane + s for s in starts], axis=1)
    key_index = lax.broadcasted_iota(jnp.int32, (rows, rows), 0)
    width = queries_ref.shape[1]
    copies = [
        pltpu.make_async_copy(ref, blocks_ref.at[pl.ds(b * rows, rows)], sems.at[b])
        for b, ref in enumerate(every)
    ]
    for copy in copies:
        copy.start()
    top_ref[...] = jnp.full(top_ref.shape, NEG_FILL, jnp.float32)
    total_ref[...] = jnp.zeros(total_ref.shape, jnp.float32)
    acc_ref[...] = jnp.zeros(acc_ref.shape, jnp.float32)
    for copy in copies:
        copy.wait()

    def block_step(b, carry):
        valid = jnp.where(b == 1, core == 1, chip >= b // 2)
        ahead = jnp.where(b == 0, 0, rows)
        block_ref = blocks_ref.at[pl.ds(pl.multiple_of(b * rows, rows), rows)]

        def tile_step(t, carry):
            cols = pl.ds(pl.multiple_of(t * rows, rows), rows)
            s = jnp.dot(block_ref[:, :HD], queries_ref[:, cols], preferred_element_type=jnp.float32)
            s = jnp.where(key_index - ahead <= row_index, s, NEG_FILL)
            top = jnp.maximum(top_ref[:, cols], jnp.max(s, axis=0, keepdims=True))
            p = jnp.exp2((s - top) * EXP2_SCALE)
            factor = jnp.exp2((top_ref[:, cols] - top) * EXP2_SCALE)
            mixed = jnp.dot(
                values_of([block_ref]), p.astype(jnp.bfloat16), preferred_element_type=jnp.float32
            )
            total_ref[:, cols] = total_ref[:, cols] * factor + mixed[HD : HD + 1]
            acc_ref[:, cols] = acc_ref[:, cols] * factor + mixed[:HD]
            top_ref[:, cols] = top
            return carry

        @pl.when(valid)
        def _():
            lax.fori_loop(0, width // rows, tile_step, 0)

        return carry

    lax.fori_loop(0, len(every), block_step, 0)


def last_kernel(groups, count, every_count, rows, parts, queries_ref, shift_ref, total_in, acc_in, *refs):
    refs = list(refs)
    blocks, refs = refs[:count], refs[count:]
    every, refs = trim(refs[:every_count], rows), refs[every_count:]
    out_refs, (total_ref, acc_ref, top_ref, blocks_ref, sems) = refs[:parts], refs[parts:]
    total_ref[...] = total_in[...]
    acc_ref[...] = acc_in[...]
    attend_groups(groups, blocks, (queries_ref, shift_ref, total_ref, acc_ref), rows)
    in_range = jnp.max(total_ref[...]) <= TOTAL_LIMIT

    @pl.when(jnp.logical_not(in_range))
    def _():
        recompute(rows, parts, queries_ref, every, total_ref, acc_ref, top_ref, blocks_ref, sems)

    piece = rows // parts

    def finish(g, carry):
        cols = pl.ds(pl.multiple_of(g * rows, rows), rows)
        out = pl.ds(pl.multiple_of(g * HD, HD), HD)
        result = (acc_ref[:, cols] * (1.0 / total_ref[:, cols])).astype(jnp.bfloat16).T
        for k in range(parts):
            out_refs[k][:, out] = result[k * piece : (k + 1) * piece]
        return carry

    lax.fori_loop(0, queries_ref.shape[1] // rows, finish, 0, unroll=True)


def attend_last(state, groups, blocks, every, rows, parts, share=1):
    queries, shift, total, acc = state
    group = queries.shape[1] // rows
    vmem, anywhere = pl.BlockSpec(memory_space=pltpu.VMEM), pl.BlockSpec(memory_space=pl.ANY)
    return pl.pallas_call(
        functools.partial(last_kernel, groups, len(blocks), len(every), rows, parts),
        in_specs=[vmem] * (4 + len(blocks)) + [anywhere] * len(every),
        out_specs=[vmem] * parts,
        out_shape=[jax.ShapeDtypeStruct((rows // parts, group * HD), jnp.bfloat16)] * parts,
        scratch_shapes=[
            pltpu.VMEM(total.shape, jnp.float32),
            pltpu.VMEM(acc.shape, jnp.float32),
            pltpu.VMEM(total.shape, jnp.float32),
            pltpu.VMEM((len(every) * rows, 2 * HD), jnp.bfloat16),
            pltpu.SemaphoreType.DMA((len(every),)),
        ],
        compiler_params=pltpu.CompilerParams(vmem_limit_bytes=LIMIT),
        cost_estimate=cost(queries.shape[1], sum(b.shape[0] for b in blocks), share),
        name="attend_last",
    )(queries, shift, total, acc, *blocks, *every)


def place_kernel(heads, parts, *refs):
    pieces, out_ref, sems = refs[: heads * parts], refs[-2], refs[-1]
    me = lax.axis_index("heads")
    copies = []
    for head in range(heads):
        for k in range(parts):
            src = pieces[head * parts + k]
            cols = src.shape[1]
            start = pl.multiple_of(((me ^ k) * heads + head) * cols, cols)
            copies.append(
                pltpu.make_async_copy(src, out_ref.at[:, pl.ds(start, cols)], sems.at[len(copies)])
            )
    for c in copies:
        c.start()
    for c in copies:
        c.wait()


def place(pieces, heads, parts):
    rows, cols = pieces[0].shape
    return pl.pallas_call(
        functools.partial(place_kernel, heads, parts),
        in_specs=[pl.BlockSpec(memory_space=pltpu.VMEM)] * len(pieces),
        out_specs=pl.BlockSpec(memory_space=pl.ANY),
        out_shape=jax.ShapeDtypeStruct((rows, cols * len(pieces)), jnp.bfloat16),
        compiler_params=pltpu.CompilerParams(vmem_limit_bytes=16 << 20),
        scratch_shapes=[pltpu.SemaphoreType.DMA((len(pieces),))],
        name="place",
    )(*pieces)


def after(value, *earlier):
    return lax.optimization_barrier((value, *earlier))[0]


class Exchange:
    def __init__(self, ctx_size, parts, group, queries, table, packs):
        self.size, self.parts, self.rows = ctx_size, parts, queries.shape[0]
        self.chips, self.heads = ctx_size // 2, range(len(packs))
        self.swap = [(c, c ^ 1) for c in range(ctx_size)]
        self.near = [[pack, self.up(pack, 1)] for pack in packs]
        self.far = [[self.across(pack)] for pack in packs]
        self.states = attend_first(queries, table, packs, group, parts)

    def across(self, block):
        return lax.ppermute(block, "ctx", self.swap)

    def up(self, block, step, cross=0):
        low = 2 * (step - 1)
        top = [(c, (c + 2 if c + 2 < self.size else low + c % 2) ^ cross) for c in range(low, self.size)]
        return lax.ppermute(block, "ctx", self.swap[:low] + top)

    def pass_on(self, head, step, *earlier):
        block = after(self.near[head][step], *earlier)
        self.near[head][step] = block
        if step + 1 < self.chips:
            self.near[head].append(self.up(block, step + 1))
        self.far[head].append(self.across(block))

    def blocks(self, head, steps):
        out = []
        for s in steps:
            out += [self.far[head][0]] if s == 0 else [self.near[head][s], self.far[head][s]]
        return out

    def state(self, head, earlier):
        queries_t, shift, total, acc = self.states[head]
        return queries_t, shift, after(total, *earlier), acc

    def call(self, head, steps, *earlier, share=1):
        state = self.state(head, earlier)
        self.states[head] = attend_next(state, steps, self.blocks(head, steps), self.rows, share)
        return self.states[head][2]

    def last(self, head, *earlier, share=1):
        every = [b for pair in zip(self.near[head], self.far[head], strict=True) for b in pair]
        steps = [self.chips - 1]
        blocks = self.blocks(head, steps)
        return attend_last(self.state(head, earlier), steps, blocks, every, self.rows, self.parts, share)

    def spread(self, outs, *earlier):
        out = [after(o, *earlier) if earlier else o for o in outs]
        perms = [[(i, i ^ k) for i in range(self.parts)] for k in range(self.parts)]
        return [outs[0]] + [lax.ppermute(out[k], "heads", perms[k]) for k in range(1, self.parts)]


def in_turn(ex):
    began = [ex.states[-1][2], *(far[0] for far in ex.far)]
    pieces = []
    for head in ex.heads:
        ex.pass_on(head, 1, *began)
        for step in range(1, ex.chips - 1):
            ex.call(head, [0, 1] if step == 1 else [step])
            ex.pass_on(head, step + 1, ex.states[head][2])
        pieces += ex.spread(ex.last(head))
    return pieces


def four_chips(ex):
    one, two = 0, 1
    latest = ex.states[two][2]
    ex.pass_on(one, 1, latest, ex.far[one][0], ex.far[two][0])
    ex.pass_on(two, 1, latest)
    latest = ex.call(one, [0, 1], latest, ex.near[one][1])
    ex.pass_on(one, 2, latest)
    latest = ex.call(one, [2], latest, share=0)
    ex.pass_on(two, 2, latest)
    ex.far[two].append(ex.up(ex.near[two][2], 3, 1))
    latest = ex.call(two, [0, 1], latest)
    ex.pass_on(one, 3, latest)
    outs = ex.last(one, latest, share=0)
    pieces = ex.spread(outs)
    latest = ex.call(two, [2], outs[0], share=0)
    outs = ex.last(two, latest)
    return pieces + ex.spread(outs, pieces[1])


def local(ctx_size, parts, queries, keys, values, positions):
    kv_heads = keys.shape[1] // HD
    group = queries.shape[1] // (kv_heads * HD)
    four = (ctx_size, kv_heads) == (8, 2)
    table, *packs = prep(keys, values, positions, (0, MORE) if four else (0,) * kv_heads)
    ex = Exchange(ctx_size, parts, group, queries, table, packs)
    pieces = four_chips(ex) if four else in_turn(ex)
    return place(pieces, kv_heads, parts)


def solution(mesh):
    return jax.shard_map(
        functools.partial(local, mesh.shape["ctx"], mesh.shape["heads"]),
        mesh=mesh,
        in_specs=(P("ctx", "heads"), P("ctx", "heads"), P("ctx", "heads"), P("ctx")),
        out_specs=P(("ctx", "heads"), None),
        check_vma=False,
    )
```

```python
import functools
import math

import jax
import jax.numpy as jnp
import numpy as np
from jax import lax
from jax.experimental import pallas as pl
from jax.experimental.pallas import tpu as pltpu
from jax.sharding import PartitionSpec as P

HD = 128
HALF = HD // 2
NEG_FILL = -1e30
EXP2_SCALE = math.log2(math.e) / math.sqrt(HD)
TOTAL_LIMIT = 2.0**100
TILE = 1536
ONES = 16
LIMIT = 24 << 20
MORE = 16


def inverse_frequencies():
    base = 500000.0 ** (-2.0 * np.arange(HALF) / HD)
    wave = 2.0 * math.pi / base
    blend = (8192.0 / wave - 1.0) / 3.0
    middle = (1.0 - blend) * base / 8.0 + blend * base
    return np.where(wave < 2048.0, base, np.where(wave > 8192.0, base / 8.0, middle)).astype(np.float32)


def frequency_row():
    lane = lax.broadcasted_iota(jnp.int32, (1, HD), 1) % HALF
    row = jnp.zeros((1, HD), jnp.float32)
    for i, freq in enumerate(inverse_frequencies()):
        row = jnp.where(lane == i, float(freq), row)
    return row


def cos_sin(angle):
    turns = jnp.round(angle * (2.0 / math.pi))
    rest = angle - turns * 1.5703125
    rest = rest - turns * 4.837512969970703e-4
    rest = rest - turns * 7.54978995489188e-8
    quadrant = turns.astype(jnp.int32) & 3
    sq = rest * rest
    sine = rest + rest * sq * (-1.6666654611e-1 + sq * (8.3321608736e-3 - sq * 1.9515295891e-4))
    cosine = (
        1.0
        - 0.5 * sq
        + sq * sq * (4.166664568298827e-2 + sq * (-1.388731625493765e-3 + sq * 2.443315711809948e-5))
    )
    odd = (quadrant & 1) == 1
    cos_out = jnp.where(odd, sine, cosine)
    sin_out = jnp.where(odd, cosine, sine)
    cos_out = jnp.where((quadrant == 1) | (quadrant == 2), -cos_out, cos_out)
    sin_out = jnp.where(quadrant >= 2, -sin_out, sin_out)
    return cos_out, sin_out


def rotate(x, cosine, sine):
    return x * cosine + pltpu.roll(x, HALF, 1) * sine


def table_kernel(pos_ref, table_ref):
    sign = jnp.where(lax.broadcasted_iota(jnp.int32, (HD, HD), 1) < HALF, -1.0, 1.0)
    freq = frequency_row()
    for at in range(0, pos_ref.shape[0], HD):
        rows = slice(at, at + HD)
        pos = pos_ref[rows].reshape(1, HD).astype(jnp.float32)
        pos = jnp.broadcast_to(pos, (HD, HD)).T
        cosine, sine = cos_sin(pos * freq)
        table_ref[rows, :HD] = cosine
        table_ref[rows, HD:] = sine * sign


def pack_kernel(heads, table_ref, k_ref, v_ref, *pack_refs):
    for at in range(0, k_ref.shape[0], HD):
        rows = slice(at, at + HD)
        for head in range(heads):
            cols = slice(head * HD, (head + 1) * HD)
            key = rotate(k_ref[rows, cols].astype(jnp.float32), table_ref[rows, :HD], table_ref[rows, HD:])
            pack_refs[head][rows, :HD] = key.astype(jnp.bfloat16)
            pack_refs[head][rows, HD:] = v_ref[rows, cols].T
    for pack_ref in pack_refs:
        if pack_ref.shape[0] > k_ref.shape[0]:
            more = slice(k_ref.shape[0], pack_ref.shape[0])
            pack_ref[more, :] = jnp.zeros((more.stop - more.start, 2 * HD), jnp.bfloat16)


def prep(keys, values, positions, extra):
    rows, cols = keys.shape
    heads = cols // HD
    vmem = pl.BlockSpec(memory_space=pltpu.VMEM)
    params = pltpu.CompilerParams(vmem_limit_bytes=16 << 20)
    table = pl.pallas_call(
        table_kernel,
        in_specs=[vmem],
        out_specs=vmem,
        out_shape=jax.ShapeDtypeStruct((rows, 2 * HD), jnp.float32),
        compiler_params=params,
        cost_estimate=pl.CostEstimate(flops=10**10, bytes_accessed=0, transcendentals=0),
        name="table",
    )(positions)
    packs = pl.pallas_call(
        functools.partial(pack_kernel, heads),
        in_specs=[vmem] * 3,
        out_specs=[vmem] * heads,
        out_shape=[jax.ShapeDtypeStruct((rows + more, 2 * HD), jnp.bfloat16) for more in extra],
        compiler_params=params,
        name="pack",
    )(table, keys, values)
    return table, *packs


def piece_starts(rows, parts):
    piece = rows // parts
    me = lax.axis_index("heads")
    return piece, [pl.multiple_of((me ^ k) * piece, piece) for k in range(parts)]


def trim(refs, rows):
    return [ref.at[pl.ds(0, rows)] if ref.shape[0] > rows else ref for ref in refs]


def values_of(blocks):
    tiles = [b[t : t + HD, HD:] for b in blocks for t in range(0, b.shape[0], HD)]
    values_t = jnp.concatenate(tiles, axis=1)
    return jnp.concatenate([values_t, jnp.ones((ONES, values_t.shape[1]), jnp.bfloat16)], axis=0)


def attend(state, blocks, allowed=None):
    queries_ref, shift_ref, total_ref, acc_ref = state
    width = queries_ref.shape[1]
    tile = min(TILE, width)

    def step(i, carry):
        cols = pl.ds(pl.multiple_of(i * tile, tile), tile)
        keys = [b[:, :HD] for b in blocks]
        keys = keys[0] if len(keys) == 1 else jnp.concatenate(keys, axis=0)
        s = jnp.dot(keys, queries_ref[:, cols], preferred_element_type=jnp.float32)
        if allowed is not None:
            s = jnp.where(jnp.concatenate([allowed] * (tile // allowed.shape[1]), 1), s, NEG_FILL)
        p = jnp.exp2(s * EXP2_SCALE - shift_ref[:, cols]).astype(jnp.bfloat16)
        mixed = jnp.dot(values_of(blocks), p, preferred_element_type=jnp.float32)
        if allowed is None:
            total_ref[:, cols] += mixed[HD : HD + 1]
            acc_ref[:, cols] += mixed[:HD]
        else:
            total_ref[:, cols] = mixed[HD : HD + 1]
            acc_ref[:, cols] = mixed[:HD]
        return carry

    lax.fori_loop(0, width // tile, step, 0)


def first_kernel(heads, group, parts, q_ref, table_ref, *refs):
    rows = q_ref.shape[0]
    own_refs, out_refs = trim(refs[:heads], rows), refs[heads:]
    piece, starts = piece_starts(rows, parts)
    table = jnp.concatenate([table_ref[pl.ds(s, piece), :] for s in starts], axis=0)
    lane = lax.broadcasted_iota(jnp.int32, (1, piece), 1)
    row_index = jnp.concatenate([lane + s for s in starts], axis=1)
    allowed = lax.broadcasted_iota(jnp.int32, (rows, rows), 0) <= row_index
    for head, own_ref in enumerate(own_refs):
        state = out_refs[4 * head : 4 * head + 4]
        queries_ref, shift_ref = state[:2]
        own_t = jnp.concatenate([own_ref[pl.ds(s, piece), :HD] for s in starts], axis=0)
        own_t = own_t.astype(jnp.float32).T
        for g in range(group):
            cols = slice((head * group + g) * HD, (head * group + g + 1) * HD)
            x = jnp.concatenate([q_ref[pl.ds(s, piece), cols] for s in starts], axis=0)
            x = rotate(x.astype(jnp.float32), table[:, :HD], table[:, HD:])
            x = x.T.astype(jnp.bfloat16)
            out = slice(g * rows, (g + 1) * rows)
            queries_ref[:, out] = x
            own_score = jnp.sum(x.astype(jnp.float32) * own_t, axis=0, keepdims=True)
            shift_ref[:, out] = own_score * EXP2_SCALE
        attend(state, [own_ref], allowed)


def attend_first(queries, table, owns, group, parts):
    rows = queries.shape[0]
    width = group * rows
    vmem = pl.BlockSpec(memory_space=pltpu.VMEM)
    flat = pl.pallas_call(
        functools.partial(first_kernel, len(owns), group, parts),
        in_specs=[vmem] * (2 + len(owns)),
        out_specs=[vmem] * (4 * len(owns)),
        out_shape=[
            jax.ShapeDtypeStruct((HD, width), jnp.bfloat16),
            jax.ShapeDtypeStruct((1, width), jnp.float32),
            jax.ShapeDtypeStruct((1, width), jnp.float32),
            jax.ShapeDtypeStruct((HD, width), jnp.float32),
        ]
        * len(owns),
        compiler_params=pltpu.CompilerParams(vmem_limit_bytes=LIMIT),
        cost_estimate=cost(width * len(owns), rows),
        name="attend_first",
    )(queries, table, *owns)
    return [tuple(flat[4 * h : 4 * h + 4]) for h in range(len(owns))]


def cost(width, keys, share=1):
    return pl.CostEstimate(flops=share * 8 * width * keys * HD, bytes_accessed=0, transcendentals=0)


def attend_groups(groups, refs, state, rows):
    rank = lax.axis_index("ctx")
    chip, core = rank // 2, rank % 2
    refs = trim(refs, rows)
    for step in groups:
        blocks = [refs.pop(0) for _ in range(1 if step == 0 else 2)]
        there = core == 1 if step == 0 else chip >= step
        pl.when(there)(functools.partial(attend, state, blocks))


def next_kernel(groups, rows, queries_ref, shift_ref, total_in, acc_in, *refs):
    del total_in, acc_in
    attend_groups(groups, refs[:-2], (queries_ref, shift_ref, refs[-2], refs[-1]), rows)


def attend_next(state, groups, blocks, rows, share=1):
    queries, shift, total, acc = state
    vmem = pl.BlockSpec(memory_space=pltpu.VMEM)
    total, acc = pl.pallas_call(
        functools.partial(next_kernel, groups, rows),
        in_specs=[vmem] * (4 + len(blocks)),
        out_specs=[vmem] * 2,
        out_shape=[jax.ShapeDtypeStruct(x.shape, x.dtype) for x in (total, acc)],
        input_output_aliases={2: 0, 3: 1},
        compiler_params=pltpu.CompilerParams(vmem_limit_bytes=LIMIT),
        cost_estimate=cost(queries.shape[1], sum(b.shape[0] for b in blocks), share),
        name="attend_next",
    )(queries, shift, total, acc, *blocks)
    return queries, shift, total, acc


def recompute(rows, parts, queries_ref, every, total_ref, acc_ref, top_ref, blocks_ref, sems):
    rank = lax.axis_index("ctx")
    chip, core = rank // 2, rank % 2
    piece, starts = piece_starts(rows, parts)
    lane = lax.broadcasted_iota(jnp.int32, (1, piece), 1)
    row_index = jnp.concatenate([lane + s for s in starts], axis=1)
    key_index = lax.broadcasted_iota(jnp.int32, (rows, rows), 0)
    width = queries_ref.shape[1]
    copies = [
        pltpu.make_async_copy(ref, blocks_ref.at[pl.ds(b * rows, rows)], sems.at[b])
        for b, ref in enumerate(every)
    ]
    for copy in copies:
        copy.start()
    top_ref[...] = jnp.full(top_ref.shape, NEG_FILL, jnp.float32)
    total_ref[...] = jnp.zeros(total_ref.shape, jnp.float32)
    acc_ref[...] = jnp.zeros(acc_ref.shape, jnp.float32)
    for copy in copies:
        copy.wait()

    def block_step(b, carry):
        valid = jnp.where(b == 1, core == 1, chip >= b // 2)
        ahead = jnp.where(b == 0, 0, rows)
        block_ref = blocks_ref.at[pl.ds(pl.multiple_of(b * rows, rows), rows)]

        def tile_step(t, carry):
            cols = pl.ds(pl.multiple_of(t * rows, rows), rows)
            s = jnp.dot(block_ref[:, :HD], queries_ref[:, cols], preferred_element_type=jnp.float32)
            s = jnp.where(key_index - ahead <= row_index, s, NEG_FILL)
            top = jnp.maximum(top_ref[:, cols], jnp.max(s, axis=0, keepdims=True))
            p = jnp.exp2((s - top) * EXP2_SCALE)
            factor = jnp.exp2((top_ref[:, cols] - top) * EXP2_SCALE)
            mixed = jnp.dot(
                values_of([block_ref]), p.astype(jnp.bfloat16), preferred_element_type=jnp.float32
            )
            total_ref[:, cols] = total_ref[:, cols] * factor + mixed[HD : HD + 1]
            acc_ref[:, cols] = acc_ref[:, cols] * factor + mixed[:HD]
            top_ref[:, cols] = top
            return carry

        @pl.when(valid)
        def _():
            lax.fori_loop(0, width // rows, tile_step, 0)

        return carry

    lax.fori_loop(0, len(every), block_step, 0)


def last_kernel(groups, count, every_count, rows, parts, queries_ref, shift_ref, total_in, acc_in, *refs):
    refs = list(refs)
    blocks, refs = refs[:count], refs[count:]
    every, refs = trim(refs[:every_count], rows), refs[every_count:]
    out_refs, (total_ref, acc_ref, top_ref, blocks_ref, sems) = refs[:parts], refs[parts:]
    total_ref[...] = total_in[...]
    acc_ref[...] = acc_in[...]
    attend_groups(groups, blocks, (queries_ref, shift_ref, total_ref, acc_ref), rows)
    in_range = jnp.max(total_ref[...]) <= TOTAL_LIMIT

    @pl.when(jnp.logical_not(in_range))
    def _():
        recompute(rows, parts, queries_ref, every, total_ref, acc_ref, top_ref, blocks_ref, sems)

    piece = rows // parts

    def finish(g, carry):
        cols = pl.ds(pl.multiple_of(g * rows, rows), rows)
        out = pl.ds(pl.multiple_of(g * HD, HD), HD)
        result = (acc_ref[:, cols] * (1.0 / total_ref[:, cols])).astype(jnp.bfloat16).T
        for k in range(parts):
            out_refs[k][:, out] = result[k * piece : (k + 1) * piece]
        return carry

    lax.fori_loop(0, queries_ref.shape[1] // rows, finish, 0, unroll=True)


def attend_last(state, groups, blocks, every, rows, parts, share=1):
    queries, shift, total, acc = state
    group = queries.shape[1] // rows
    vmem, anywhere = pl.BlockSpec(memory_space=pltpu.VMEM), pl.BlockSpec(memory_space=pl.ANY)
    return pl.pallas_call(
        functools.partial(last_kernel, groups, len(blocks), len(every), rows, parts),
        in_specs=[vmem] * (4 + len(blocks)) + [anywhere] * len(every),
        out_specs=[vmem] * parts,
        out_shape=[jax.ShapeDtypeStruct((rows // parts, group * HD), jnp.bfloat16)] * parts,
        scratch_shapes=[
            pltpu.VMEM(total.shape, jnp.float32),
            pltpu.VMEM(acc.shape, jnp.float32),
            pltpu.VMEM(total.shape, jnp.float32),
            pltpu.VMEM((len(every) * rows, 2 * HD), jnp.bfloat16),
            pltpu.SemaphoreType.DMA((len(every),)),
        ],
        compiler_params=pltpu.CompilerParams(vmem_limit_bytes=LIMIT),
        cost_estimate=cost(queries.shape[1], sum(b.shape[0] for b in blocks), share),
        name="attend_last",
    )(queries, shift, total, acc, *blocks, *every)


def turns(parts):
    return [0] + sorted(range(1, parts), key=lambda k: (-bin(k).count("1"), k))


def place_kernel(heads, parts, *refs):
    pieces, out_ref, sems = refs[: heads * parts], refs[-2], refs[-1]
    me = lax.axis_index("heads")
    copies = []
    for head in range(heads):
        for i, k in enumerate(turns(parts)):
            src = pieces[head * parts + i]
            cols = src.shape[1]
            start = pl.multiple_of(((me ^ k) * heads + head) * cols, cols)
            copies.append(
                pltpu.make_async_copy(src, out_ref.at[:, pl.ds(start, cols)], sems.at[len(copies)])
            )
    for c in copies:
        c.start()
    for c in copies:
        c.wait()


def place(pieces, heads, parts):
    rows, cols = pieces[0].shape
    return pl.pallas_call(
        functools.partial(place_kernel, heads, parts),
        in_specs=[pl.BlockSpec(memory_space=pltpu.VMEM)] * len(pieces),
        out_specs=pl.BlockSpec(memory_space=pl.ANY),
        out_shape=jax.ShapeDtypeStruct((rows, cols * len(pieces)), jnp.bfloat16),
        compiler_params=pltpu.CompilerParams(vmem_limit_bytes=16 << 20),
        scratch_shapes=[pltpu.SemaphoreType.DMA((len(pieces),))],
        name="place",
    )(*pieces)


def after(value, *earlier):
    return lax.optimization_barrier((value, *earlier))[0]


class Exchange:
    def __init__(self, ctx_size, parts, group, queries, table, packs):
        self.size, self.parts, self.rows = ctx_size, parts, queries.shape[0]
        self.chips, self.heads = ctx_size // 2, range(len(packs))
        self.swap = [(c, c ^ 1) for c in range(ctx_size)]
        self.near = [[pack, self.up(pack, 1)] for pack in packs]
        self.far = [[self.across(pack)] for pack in packs]
        self.states = attend_first(queries, table, packs, group, parts)

    def across(self, block):
        return lax.ppermute(block, "ctx", self.swap)

    def up(self, block, step, cross=0):
        low = 2 * (step - 1)
        top = [(c, (c + 2 if c + 2 < self.size else low + c % 2) ^ cross) for c in range(low, self.size)]
        return lax.ppermute(block, "ctx", self.swap[:low] + top)

    def pass_on(self, head, step, *earlier):
        block = after(self.near[head][step], *earlier)
        self.near[head][step] = block
        if step + 1 < self.chips:
            self.near[head].append(self.up(block, step + 1))
        self.far[head].append(self.across(block))

    def blocks(self, head, steps):
        out = []
        for s in steps:
            out += [self.far[head][0]] if s == 0 else [self.near[head][s], self.far[head][s]]
        return out

    def state(self, head, earlier):
        queries_t, shift, total, acc = self.states[head]
        return queries_t, shift, after(total, *earlier), acc

    def call(self, head, steps, *earlier, share=1):
        state = self.state(head, earlier)
        self.states[head] = attend_next(state, steps, self.blocks(head, steps), self.rows, share)
        return self.states[head][2]

    def last(self, head, *earlier, share=1):
        every = [b for pair in zip(self.near[head], self.far[head], strict=True) for b in pair]
        steps = [self.chips - 1]
        blocks = self.blocks(head, steps)
        return attend_last(self.state(head, earlier), steps, blocks, every, self.rows, self.parts, share)

    def spread(self, outs, *earlier):
        out = [after(o, *earlier) if earlier else o for o in outs]
        perms = [[(i, i ^ k) for i in range(self.parts)] for k in range(self.parts)]
        return [lax.ppermute(out[k], "heads", perms[k]) if k else outs[0] for k in turns(self.parts)]


def in_turn(ex):
    began = [ex.states[-1][2], *(far[0] for far in ex.far)]
    pieces = []
    for head in ex.heads:
        ex.pass_on(head, 1, *began)
        for step in range(1, ex.chips - 1):
            ex.call(head, [0, 1] if step == 1 else [step])
            ex.pass_on(head, step + 1, ex.states[head][2])
        pieces += ex.spread(ex.last(head))
    return pieces


def four_chips(ex):
    one, two = 0, 1
    latest = ex.states[two][2]
    ex.pass_on(one, 1, latest, ex.far[one][0], ex.far[two][0])
    ex.pass_on(two, 1, latest)
    latest = ex.call(one, [0, 1], latest, ex.near[one][1])
    ex.pass_on(one, 2, latest)
    latest = ex.call(one, [2], latest, share=0)
    ex.pass_on(two, 2, latest)
    ex.far[two].append(ex.up(ex.near[two][2], 3, 1))
    latest = ex.call(two, [1], latest)
    ex.pass_on(one, 3, latest)
    latest = ex.call(two, [0], latest, share=0)
    outs = ex.last(one, latest, share=0)
    pieces = ex.spread(outs)
    latest = ex.call(two, [2], outs[0], share=0)
    outs = ex.last(two, latest)
    return pieces + ex.spread(outs, pieces[1])


def local(ctx_size, parts, queries, keys, values, positions):
    kv_heads = keys.shape[1] // HD
    group = queries.shape[1] // (kv_heads * HD)
    four = (ctx_size, kv_heads) == (8, 2)
    table, *packs = prep(keys, values, positions, (0, MORE) if four else (0,) * kv_heads)
    ex = Exchange(ctx_size, parts, group, queries, table, packs)
    pieces = four_chips(ex) if four else in_turn(ex)
    return place(pieces, kv_heads, parts)


def solution(mesh):
    return jax.shard_map(
        functools.partial(local, mesh.shape["ctx"], mesh.shape["heads"]),
        mesh=mesh,
        in_specs=(P("ctx", "heads"), P("ctx", "heads"), P("ctx", "heads"), P("ctx")),
        out_specs=P(("ctx", "heads"), None),
        check_vma=False,
    )
```

```python
import functools
import math

import jax
import jax.numpy as jnp
import numpy as np
from jax import lax
from jax.experimental import pallas as pl
from jax.experimental.pallas import tpu as pltpu
from jax.sharding import PartitionSpec as P

HD = 128
HALF = HD // 2
NEG_FILL = -1e30
EXP2_SCALE = math.log2(math.e) / math.sqrt(HD)
TOTAL_LIMIT = 2.0**100
TILE = 1536
ONES = 16
LIMIT = 24 << 20
MORE = 16


def inverse_frequencies():
    base = 500000.0 ** (-2.0 * np.arange(HALF) / HD)
    wave = 2.0 * math.pi / base
    blend = (8192.0 / wave - 1.0) / 3.0
    middle = (1.0 - blend) * base / 8.0 + blend * base
    return np.where(wave < 2048.0, base, np.where(wave > 8192.0, base / 8.0, middle)).astype(np.float32)


def frequency_row():
    lane = lax.broadcasted_iota(jnp.int32, (1, HD), 1) % HALF
    row = jnp.zeros((1, HD), jnp.float32)
    for i, freq in enumerate(inverse_frequencies()):
        row = jnp.where(lane == i, float(freq), row)
    return row


def cos_sin(angle):
    turns = jnp.round(angle * (2.0 / math.pi))
    rest = angle - turns * 1.5703125
    rest = rest - turns * 4.837512969970703e-4
    rest = rest - turns * 7.54978995489188e-8
    quadrant = turns.astype(jnp.int32) & 3
    sq = rest * rest
    sine = rest + rest * sq * (-1.6666654611e-1 + sq * (8.3321608736e-3 - sq * 1.9515295891e-4))
    cosine = (
        1.0
        - 0.5 * sq
        + sq * sq * (4.166664568298827e-2 + sq * (-1.388731625493765e-3 + sq * 2.443315711809948e-5))
    )
    odd = (quadrant & 1) == 1
    cos_out = jnp.where(odd, sine, cosine)
    sin_out = jnp.where(odd, cosine, sine)
    cos_out = jnp.where((quadrant == 1) | (quadrant == 2), -cos_out, cos_out)
    sin_out = jnp.where(quadrant >= 2, -sin_out, sin_out)
    return cos_out, sin_out


def rotate(x, cosine, sine):
    return x * cosine + pltpu.roll(x, HALF, 1) * sine


def table_kernel(pos_ref, table_ref):
    sign = jnp.where(lax.broadcasted_iota(jnp.int32, (HD, HD), 1) < HALF, -1.0, 1.0)
    freq = frequency_row()
    for at in range(0, pos_ref.shape[0], HD):
        rows = slice(at, at + HD)
        pos = pos_ref[rows].reshape(1, HD).astype(jnp.float32)
        pos = jnp.broadcast_to(pos, (HD, HD)).T
        cosine, sine = cos_sin(pos * freq)
        table_ref[rows, :HD] = cosine
        table_ref[rows, HD:] = sine * sign


def pack_kernel(heads, table_ref, k_ref, v_ref, *pack_refs):
    for at in range(0, k_ref.shape[0], HD):
        rows = slice(at, at + HD)
        for head in range(heads):
            cols = slice(head * HD, (head + 1) * HD)
            key = rotate(k_ref[rows, cols].astype(jnp.float32), table_ref[rows, :HD], table_ref[rows, HD:])
            pack_refs[head][rows, :HD] = key.astype(jnp.bfloat16)
            pack_refs[head][rows, HD:] = v_ref[rows, cols].T
    for pack_ref in pack_refs:
        if pack_ref.shape[0] > k_ref.shape[0]:
            more = slice(k_ref.shape[0], pack_ref.shape[0])
            pack_ref[more, :] = jnp.zeros((more.stop - more.start, 2 * HD), jnp.bfloat16)


def prep(keys, values, positions, extra):
    rows, cols = keys.shape
    heads = cols // HD
    vmem = pl.BlockSpec(memory_space=pltpu.VMEM)
    params = pltpu.CompilerParams(vmem_limit_bytes=16 << 20)
    table = pl.pallas_call(
        table_kernel,
        in_specs=[vmem],
        out_specs=vmem,
        out_shape=jax.ShapeDtypeStruct((rows, 2 * HD), jnp.float32),
        compiler_params=params,
        cost_estimate=pl.CostEstimate(flops=10**10, bytes_accessed=0, transcendentals=0),
        name="table",
    )(positions)
    packs = pl.pallas_call(
        functools.partial(pack_kernel, heads),
        in_specs=[vmem] * 3,
        out_specs=[vmem] * heads,
        out_shape=[jax.ShapeDtypeStruct((rows + more, 2 * HD), jnp.bfloat16) for more in extra],
        compiler_params=params,
        name="pack",
    )(table, keys, values)
    return table, *packs


def piece_starts(rows, parts):
    piece = rows // parts
    me = lax.axis_index("heads")
    return piece, [pl.multiple_of((me ^ k) * piece, piece) for k in range(parts)]


def trim(refs, rows):
    return [ref.at[pl.ds(0, rows)] if ref.shape[0] > rows else ref for ref in refs]


def values_of(blocks):
    tiles = [b[t : t + HD, HD:] for b in blocks for t in range(0, b.shape[0], HD)]
    values_t = jnp.concatenate(tiles, axis=1)
    return jnp.concatenate([values_t, jnp.ones((ONES, values_t.shape[1]), jnp.bfloat16)], axis=0)


def attend(state, blocks, allowed=None):
    queries_ref, shift_ref, total_ref, acc_ref = state
    width = queries_ref.shape[1]
    tile = min(TILE, width)

    def step(i, carry):
        cols = pl.ds(pl.multiple_of(i * tile, tile), tile)
        keys = [b[:, :HD] for b in blocks]
        keys = keys[0] if len(keys) == 1 else jnp.concatenate(keys, axis=0)
        s = jnp.dot(keys, queries_ref[:, cols], preferred_element_type=jnp.float32)
        if allowed is not None:
            s = jnp.where(jnp.concatenate([allowed] * (tile // allowed.shape[1]), 1), s, NEG_FILL)
        p = jnp.exp2(s * EXP2_SCALE - shift_ref[:, cols]).astype(jnp.bfloat16)
        mixed = jnp.dot(values_of(blocks), p, preferred_element_type=jnp.float32)
        if allowed is None:
            total_ref[:, cols] += mixed[HD : HD + 1]
            acc_ref[:, cols] += mixed[:HD]
        else:
            total_ref[:, cols] = mixed[HD : HD + 1]
            acc_ref[:, cols] = mixed[:HD]
        return carry

    lax.fori_loop(0, width // tile, step, 0, unroll=True)


def first_kernel(heads, group, parts, q_ref, table_ref, *refs):
    rows = q_ref.shape[0]
    own_refs, out_refs = trim(refs[:heads], rows), refs[heads:]
    piece, starts = piece_starts(rows, parts)
    table = jnp.concatenate([table_ref[pl.ds(s, piece), :] for s in starts], axis=0)
    lane = lax.broadcasted_iota(jnp.int32, (1, piece), 1)
    row_index = jnp.concatenate([lane + s for s in starts], axis=1)
    allowed = lax.broadcasted_iota(jnp.int32, (rows, rows), 0) <= row_index
    for head, own_ref in enumerate(own_refs):
        state = out_refs[4 * head : 4 * head + 4]
        queries_ref, shift_ref = state[:2]
        own_t = jnp.concatenate([own_ref[pl.ds(s, piece), :HD] for s in starts], axis=0)
        own_t = own_t.astype(jnp.float32).T
        for g in range(group):
            cols = slice((head * group + g) * HD, (head * group + g + 1) * HD)
            x = jnp.concatenate([q_ref[pl.ds(s, piece), cols] for s in starts], axis=0)
            x = rotate(x.astype(jnp.float32), table[:, :HD], table[:, HD:])
            x = x.T.astype(jnp.bfloat16)
            out = slice(g * rows, (g + 1) * rows)
            queries_ref[:, out] = x
            own_score = jnp.sum(x.astype(jnp.float32) * own_t, axis=0, keepdims=True)
            shift_ref[:, out] = own_score * EXP2_SCALE
        attend(state, [own_ref], allowed)


def attend_first(queries, table, owns, group, parts):
    rows = queries.shape[0]
    width = group * rows
    vmem = pl.BlockSpec(memory_space=pltpu.VMEM)
    flat = pl.pallas_call(
        functools.partial(first_kernel, len(owns), group, parts),
        in_specs=[vmem] * (2 + len(owns)),
        out_specs=[vmem] * (4 * len(owns)),
        out_shape=[
            jax.ShapeDtypeStruct((HD, width), jnp.bfloat16),
            jax.ShapeDtypeStruct((1, width), jnp.float32),
            jax.ShapeDtypeStruct((1, width), jnp.float32),
            jax.ShapeDtypeStruct((HD, width), jnp.float32),
        ]
        * len(owns),
        compiler_params=pltpu.CompilerParams(vmem_limit_bytes=LIMIT),
        cost_estimate=cost(width * len(owns), rows),
        name="attend_first",
    )(queries, table, *owns)
    return [tuple(flat[4 * h : 4 * h + 4]) for h in range(len(owns))]


def cost(width, keys, share=1):
    return pl.CostEstimate(flops=share * 8 * width * keys * HD, bytes_accessed=0, transcendentals=0)


def attend_groups(groups, refs, state, rows):
    rank = lax.axis_index("ctx")
    chip, core = rank // 2, rank % 2
    refs = trim(refs, rows)
    for step in groups:
        blocks = [refs.pop(0) for _ in range(1 if step == 0 else 2)]
        there = core == 1 if step == 0 else chip >= step
        pl.when(there)(functools.partial(attend, state, blocks))


def next_kernel(groups, rows, queries_ref, shift_ref, total_in, acc_in, *refs):
    del total_in, acc_in
    attend_groups(groups, refs[:-2], (queries_ref, shift_ref, refs[-2], refs[-1]), rows)


def attend_next(state, groups, blocks, rows, share=1):
    queries, shift, total, acc = state
    vmem = pl.BlockSpec(memory_space=pltpu.VMEM)
    total, acc = pl.pallas_call(
        functools.partial(next_kernel, groups, rows),
        in_specs=[vmem] * (4 + len(blocks)),
        out_specs=[vmem] * 2,
        out_shape=[jax.ShapeDtypeStruct(x.shape, x.dtype) for x in (total, acc)],
        input_output_aliases={2: 0, 3: 1},
        compiler_params=pltpu.CompilerParams(vmem_limit_bytes=LIMIT),
        cost_estimate=cost(queries.shape[1], sum(b.shape[0] for b in blocks), share),
        name="attend_next",
    )(queries, shift, total, acc, *blocks)
    return queries, shift, total, acc


def recompute(rows, parts, queries_ref, every, total_ref, acc_ref, top_ref, blocks_ref, sems):
    rank = lax.axis_index("ctx")
    chip, core = rank // 2, rank % 2
    piece, starts = piece_starts(rows, parts)
    lane = lax.broadcasted_iota(jnp.int32, (1, piece), 1)
    row_index = jnp.concatenate([lane + s for s in starts], axis=1)
    key_index = lax.broadcasted_iota(jnp.int32, (rows, rows), 0)
    width = queries_ref.shape[1]
    copies = [
        pltpu.make_async_copy(ref, blocks_ref.at[pl.ds(b * rows, rows)], sems.at[b])
        for b, ref in enumerate(every)
    ]
    for copy in copies:
        copy.start()
    top_ref[...] = jnp.full(top_ref.shape, NEG_FILL, jnp.float32)
    total_ref[...] = jnp.zeros(total_ref.shape, jnp.float32)
    acc_ref[...] = jnp.zeros(acc_ref.shape, jnp.float32)
    for copy in copies:
        copy.wait()

    def block_step(b, carry):
        valid = jnp.where(b == 1, core == 1, chip >= b // 2)
        ahead = jnp.where(b == 0, 0, rows)
        block_ref = blocks_ref.at[pl.ds(pl.multiple_of(b * rows, rows), rows)]

        def tile_step(t, carry):
            cols = pl.ds(pl.multiple_of(t * rows, rows), rows)
            s = jnp.dot(block_ref[:, :HD], queries_ref[:, cols], preferred_element_type=jnp.float32)
            s = jnp.where(key_index - ahead <= row_index, s, NEG_FILL)
            top = jnp.maximum(top_ref[:, cols], jnp.max(s, axis=0, keepdims=True))
            p = jnp.exp2((s - top) * EXP2_SCALE)
            factor = jnp.exp2((top_ref[:, cols] - top) * EXP2_SCALE)
            mixed = jnp.dot(
                values_of([block_ref]), p.astype(jnp.bfloat16), preferred_element_type=jnp.float32
            )
            total_ref[:, cols] = total_ref[:, cols] * factor + mixed[HD : HD + 1]
            acc_ref[:, cols] = acc_ref[:, cols] * factor + mixed[:HD]
            top_ref[:, cols] = top
            return carry

        @pl.when(valid)
        def _():
            lax.fori_loop(0, width // rows, tile_step, 0)

        return carry

    lax.fori_loop(0, len(every), block_step, 0)


def last_kernel(groups, count, every_count, rows, parts, queries_ref, shift_ref, total_in, acc_in, *refs):
    refs = list(refs)
    blocks, refs = refs[:count], refs[count:]
    every, refs = trim(refs[:every_count], rows), refs[every_count:]
    out_refs, (total_ref, acc_ref, top_ref, blocks_ref, sems) = refs[:parts], refs[parts:]
    total_ref[...] = total_in[...]
    acc_ref[...] = acc_in[...]
    attend_groups(groups, blocks, (queries_ref, shift_ref, total_ref, acc_ref), rows)
    in_range = jnp.max(total_ref[...]) <= TOTAL_LIMIT

    @pl.when(jnp.logical_not(in_range))
    def _():
        recompute(rows, parts, queries_ref, every, total_ref, acc_ref, top_ref, blocks_ref, sems)

    piece = rows // parts

    def finish(g, carry):
        cols = pl.ds(pl.multiple_of(g * rows, rows), rows)
        out = pl.ds(pl.multiple_of(g * HD, HD), HD)
        result = (acc_ref[:, cols] * (1.0 / total_ref[:, cols])).astype(jnp.bfloat16).T
        for k in range(parts):
            out_refs[k][:, out] = result[k * piece : (k + 1) * piece]
        return carry

    lax.fori_loop(0, queries_ref.shape[1] // rows, finish, 0, unroll=True)


def attend_last(state, groups, blocks, every, rows, parts, share=1):
    queries, shift, total, acc = state
    group = queries.shape[1] // rows
    vmem, anywhere = pl.BlockSpec(memory_space=pltpu.VMEM), pl.BlockSpec(memory_space=pl.ANY)
    return pl.pallas_call(
        functools.partial(last_kernel, groups, len(blocks), len(every), rows, parts),
        in_specs=[vmem] * (4 + len(blocks)) + [anywhere] * len(every),
        out_specs=[vmem] * parts,
        out_shape=[jax.ShapeDtypeStruct((rows // parts, group * HD), jnp.bfloat16)] * parts,
        scratch_shapes=[
            pltpu.VMEM(total.shape, jnp.float32),
            pltpu.VMEM(acc.shape, jnp.float32),
            pltpu.VMEM(total.shape, jnp.float32),
            pltpu.VMEM((len(every) * rows, 2 * HD), jnp.bfloat16),
            pltpu.SemaphoreType.DMA((len(every),)),
        ],
        compiler_params=pltpu.CompilerParams(vmem_limit_bytes=LIMIT),
        cost_estimate=cost(queries.shape[1], sum(b.shape[0] for b in blocks), share),
        name="attend_last",
    )(queries, shift, total, acc, *blocks, *every)


def turns(parts):
    return [0] + sorted(range(1, parts), key=lambda k: (-bin(k).count("1"), k))


def place_kernel(heads, parts, head, *refs):
    pieces, out_ref, sems = refs[-2 - parts : -2], refs[-2], refs[-1]
    me = lax.axis_index("heads")
    copies = []
    for i, k in enumerate(turns(parts)):
        cols = pieces[i].shape[1]
        start = pl.multiple_of(((me ^ k) * heads + head) * cols, cols)
        copies.append(pltpu.make_async_copy(pieces[i], out_ref.at[:, pl.ds(start, cols)], sems.at[i]))
    for c in copies:
        c.start()
    for c in copies:
        c.wait()


def place(pieces, heads, parts):
    rows, cols = pieces[0].shape
    vmem, anywhere = pl.BlockSpec(memory_space=pltpu.VMEM), pl.BlockSpec(memory_space=pl.ANY)
    out = ()
    for head in range(heads):
        out = (
            pl.pallas_call(
                functools.partial(place_kernel, heads, parts, head),
                in_specs=[anywhere] * len(out) + [vmem] * parts,
                out_specs=anywhere,
                out_shape=jax.ShapeDtypeStruct((rows, cols * heads * parts), jnp.bfloat16),
                input_output_aliases={0: 0} if out else {},
                compiler_params=pltpu.CompilerParams(vmem_limit_bytes=16 << 20),
                scratch_shapes=[pltpu.SemaphoreType.DMA((parts,))],
                name="place",
            )(*out, *pieces[head * parts : (head + 1) * parts]),
        )
    return out[0]


def after(value, *earlier):
    return lax.optimization_barrier((value, *earlier))[0]


class Exchange:
    def __init__(self, ctx_size, parts, group, queries, table, packs):
        self.size, self.parts, self.rows = ctx_size, parts, queries.shape[0]
        self.chips, self.heads = ctx_size // 2, range(len(packs))
        self.swap = [(c, c ^ 1) for c in range(ctx_size)]
        self.near = [[pack, self.up(pack, 1)] for pack in packs]
        self.far = [[self.across(pack)] for pack in packs]
        self.states = attend_first(queries, table, packs, group, parts)

    def across(self, block):
        return lax.ppermute(block, "ctx", self.swap)

    def up(self, block, step, cross=0):
        low = 2 * (step - 1)
        top = [(c, (c + 2 if c + 2 < self.size else low + c % 2) ^ cross) for c in range(low, self.size)]
        return lax.ppermute(block, "ctx", self.swap[:low] + top)

    def pass_on(self, head, step, *earlier):
        block = after(self.near[head][step], *earlier)
        self.near[head][step] = block
        if step + 1 < self.chips:
            self.near[head].append(self.up(block, step + 1))
        self.far[head].append(self.across(block))

    def blocks(self, head, steps):
        out = []
        for s in steps:
            out += [self.far[head][0]] if s == 0 else [self.near[head][s], self.far[head][s]]
        return out

    def state(self, head, earlier):
        queries_t, shift, total, acc = self.states[head]
        return queries_t, shift, after(total, *earlier), acc

    def call(self, head, steps, *earlier, share=1):
        state = self.state(head, earlier)
        self.states[head] = attend_next(state, steps, self.blocks(head, steps), self.rows, share)
        return self.states[head][2]

    def last(self, head, *earlier, share=1):
        every = [b for pair in zip(self.near[head], self.far[head], strict=True) for b in pair]
        steps = [self.chips - 1]
        blocks = self.blocks(head, steps)
        return attend_last(self.state(head, earlier), steps, blocks, every, self.rows, self.parts, share)

    def spread(self, outs, *earlier):
        out = [after(o, *earlier) if earlier else o for o in outs]
        perms = [[(i, i ^ k) for i in range(self.parts)] for k in range(self.parts)]
        return [lax.ppermute(out[k], "heads", perms[k]) if k else outs[0] for k in turns(self.parts)]


def in_turn(ex):
    began = [ex.states[-1][2], *(far[0] for far in ex.far)]
    pieces = []
    for head in ex.heads:
        ex.pass_on(head, 1, *began)
        for step in range(1, ex.chips - 1):
            ex.call(head, [0, 1] if step == 1 else [step])
            ex.pass_on(head, step + 1, ex.states[head][2])
        pieces += ex.spread(ex.last(head))
    return pieces


def four_chips(ex):
    one, two = 0, 1
    latest = ex.states[two][2]
    ex.pass_on(one, 1, latest, ex.far[one][0], ex.far[two][0])
    ex.pass_on(two, 1, latest)
    latest = ex.call(one, [0, 1], latest, ex.near[one][1])
    ex.pass_on(one, 2, latest)
    latest = ex.call(one, [2], latest, share=0)
    ex.pass_on(two, 2, latest)
    ex.far[two].append(ex.up(ex.near[two][2], 3, 1))
    latest = ex.call(two, [1], latest)
    ex.pass_on(one, 3, latest)
    latest = ex.call(two, [0], latest, share=0)
    outs = ex.last(one, latest, share=0)
    pieces = ex.spread(outs)
    latest = ex.call(two, [2], outs[0], share=0)
    outs = ex.last(two, latest)
    return pieces + ex.spread(outs, pieces[1])


def local(ctx_size, parts, queries, keys, values, positions):
    kv_heads = keys.shape[1] // HD
    group = queries.shape[1] // (kv_heads * HD)
    four = (ctx_size, kv_heads) == (8, 2)
    table, *packs = prep(keys, values, positions, (0, MORE) if four else (0,) * kv_heads)
    ex = Exchange(ctx_size, parts, group, queries, table, packs)
    pieces = four_chips(ex) if four else in_turn(ex)
    return place(pieces, kv_heads, parts)


def solution(mesh):
    return jax.shard_map(
        functools.partial(local, mesh.shape["ctx"], mesh.shape["heads"]),
        mesh=mesh,
        in_specs=(P("ctx", "heads"), P("ctx", "heads"), P("ctx", "heads"), P("ctx")),
        out_specs=P(("ctx", "heads"), None),
        check_vma=False,
    )
```
